32 devices in a mesh: dp: 8 (over z, y), mp: 4 (over x, core).
Axes of the slice: x: 2, y: 2, z: 4, core: 2. Of those that a mesh axis runs over, the one named last changes fastest.
Arguments:
- tokens: bfloat16 [128, 128, 1024], P('dp', 'mp'), may hold values from -6 to 6
- cotangent: bfloat16 [128, 128, 1024], P('dp', 'mp'), may hold values from -6 to 6
- block_lang: int32 [128], P('dp'), may hold values from 0 to 15, as said below
- counts: int32 [128], P('dp'), may hold values from 1 to 128, as said below
- slot_of: int32 [16], replicated, may hold values from 0 to 15, as said below
- ln_gain: bfloat16 [1024, 16], P('mp', 'dp'), may hold values from 0.099609375 to 1.8984375
- w_down: bfloat16 [1024, 16, 512], P('mp', 'dp'), may hold values from -0.1875 to 0.1875
- w_up: bfloat16 [1024, 16, 512], P('mp', 'dp'), may hold values from -0.25 to 0.25
Outputs:
- token_grad: bfloat16 [128, 128, 1024], P('dp', 'mp')
- grad_down: bfloat16 [1024, 16, 512], P('mp', 'dp')
- grad_up: bfloat16 [1024, 16, 512], P('mp', 'dp')
The draws below stay inside these ranges and needn't reach their ends.
Inputs may be any that keep to these rules, and one draw needn't show every extreme that they name: A permutation: language g's adapter is stored at index slot_of[g], on index slot_of[g] // 2 of dp. `block_lang`: with owner(g) = slot_of[g] // 2, at most 2 blocks of one index of dp name languages of one owner; in every draw some owner receives 2 blocks from every index of dp. `counts`: some block of every index of dp has all 128 rows live.
All inputs are finite; a program needn't handle non-finite values.
Results may differ from the reference program's by a relative error of at most 0.0062.
Values may be sent and summed in bfloat16 or wider, within the bound.
No kernel may reach another device: no remote copies, remote signals or barrier semaphores. Data moves between devices by JAX's collectives and lax.ppermute only.
A program may use at most 128 MiB of HBM per device.

```python
import jax
import jax.numpy as jnp
from jax import lax

D = 1024
B = 512
LANG_DEV = 2
BLK = 128
BLOCKS_DEV = 16
LANGS = 16
NB = 128
CAP = 2
N_DP = 8


def block_plan(key):
    slot_table = jax.random.permutation(jax.random.fold_in(key, 11), LANGS).astype(jnp.int32)
    lang_at = jnp.argsort(slot_table, stable=True).astype(jnp.int32)
    hot_order = jax.random.permutation(jax.random.fold_in(key, 12), N_DP)
    hot_count = max(1, BLOCKS_DEV // (2 * CAP))
    cand_owner = jnp.arange(N_DP * CAP) // CAP
    is_hot = (hot_order[cand_owner] < hot_count).astype(jnp.int32)
    random_part = jax.random.randint(jax.random.fold_in(key, 13), (N_DP, N_DP * CAP), 0, 1 << 20)
    scores = (random_part + is_hot[None, :] * (1 << 21)) * (N_DP * CAP) + jnp.arange(N_DP * CAP)[None, :]
    chosen = lax.top_k(scores, BLOCKS_DEV)[1]
    owner_ids = chosen // CAP
    local_ids = jax.random.randint(jax.random.fold_in(key, 14), (N_DP, BLOCKS_DEV), 0, LANG_DEV)
    languages = lang_at[owner_ids * LANG_DEV + local_ids]
    return (slot_table, languages.reshape(N_DP * BLOCKS_DEV).astype(jnp.int32))


def draw_slot_of(key, part):
    return block_plan(key)[0]


def draw_block_lang(key, part):
    return block_plan(key)[1]


def draw_counts(key, part):
    lengths = jax.random.randint(key, (N_DP * BLOCKS_DEV,), 1, BLK + 1)
    first_block = jnp.arange(N_DP * BLOCKS_DEV) % BLOCKS_DEV == 0
    return jnp.where(first_block, BLK, lengths).astype(jnp.int32)


def block_scale(key, extent, split, low, largest):
    loudness, own = 1.0, jax.random.fold_in(key, 6)
    for dim, shards_of in split:
        heights = jnp.exp(jax.random.uniform(jax.random.fold_in(own, dim), (shards_of,), jnp.float32, low / len(split), largest / len(split)))
        loudness = loudness * jnp.repeat(heights, extent[dim] // shards_of).reshape([-1 if axis == dim else 1 for axis in range(len(extent))])
    return loudness


def bell_draw(rng, extent, deviation, limit, split=(), kind=jnp.bfloat16):
    array = deviation * jax.random.normal(rng, extent, jnp.float32)
    if split:
        array = array * block_scale(rng, extent, split, -0.22, 0.18)
    return jnp.clip(array, -limit, limit).astype(kind)


def setup_inputs(seed: int = 0) -> dict:
    key_of = jax.random.split(jax.random.key(seed), 9)
    tokens = bell_draw(key_of[0], (NB, BLK, D), 1.0, 6.0, ((0, 8), (1, 4)))
    cotangent = bell_draw(key_of[1], (NB, BLK, D), 1.0, 6.0, ((0, 8), (1, 4)))
    block_lang = draw_block_lang(jax.random.fold_in(key_of[8], 71), 0)
    counts = draw_counts(jax.random.fold_in(key_of[8], 71), 0)
    slot_of = draw_slot_of(jax.random.fold_in(key_of[8], 71), 0)
    ln_gain = jnp.clip(1.0 + 0.18 * jax.random.normal(key_of[5], (D, LANGS), jnp.float32), 0.099609375, 1.8984375).astype(jnp.bfloat16)
    w_down = bell_draw(key_of[6], (D, LANGS, B), D ** -0.5, 0.1875, ((0, 4), (1, 8)))
    w_up = bell_draw(key_of[7], (D, LANGS, B), B ** -0.5, 0.25, ((0, 4), (1, 8)))
    return dict(tokens=tokens, cotangent=cotangent, block_lang=block_lang, counts=counts, slot_of=slot_of, ln_gain=ln_gain, w_down=w_down, w_up=w_up)


def exact_gelu(values):
    return jax.nn.gelu(values, approximate=False)

def adapter_backward(inputs, cotan, live_rows, gains, down_cols, up_cols):
    values = inputs.astype(jnp.float32)
    row_mean = lax.optimization_barrier(jnp.mean(values, axis=-1, keepdims=True))
    centered = values - row_mean
    inv_std = lax.rsqrt(lax.optimization_barrier(jnp.mean(centered * centered, axis=-1, keepdims=True)) + 1e-05)
    unit_rows = centered * inv_std
    gain_row = gains.astype(jnp.float32)[None, :]
    normed = (unit_rows * gain_row).astype(jnp.bfloat16)
    inner = jnp.dot(normed, down_cols, preferred_element_type=jnp.float32)
    activation, gelu_back = jax.vjp(exact_gelu, inner)
    act_low = activation.astype(jnp.bfloat16)
    masked = jnp.where(live_rows[:, None], cotan, jnp.zeros((), cotan.dtype))
    grad_act = jnp.dot(masked, up_cols, preferred_element_type=jnp.float32)
    grad_inner = gelu_back(grad_act)[0].astype(jnp.bfloat16)
    grad_normed = lax.dot_general(grad_inner, down_cols, (((1,), (1,)), ((), ())), preferred_element_type=jnp.float32)
    scaled = grad_normed * gain_row
    token_grad = masked.astype(jnp.float32) + inv_std * (scaled - lax.optimization_barrier(jnp.mean(scaled, axis=-1, keepdims=True)) - unit_rows * lax.optimization_barrier(jnp.mean(scaled * unit_rows, axis=-1, keepdims=True)))
    return (token_grad.astype(jnp.bfloat16), normed, act_low, grad_inner, masked)

def reference(tokens, cotangent, block_lang, counts, slot_of, ln_gain, w_down, w_up):
    slot_ids = slot_of[block_lang].astype(jnp.int32)
    zero_index = jnp.zeros((), jnp.int32)
    row_index = jnp.arange(BLK, dtype=jnp.int32)

    def one_block(totals, inputs_now):
        block_x, block_dy, slot_now, count_now = inputs_now
        gains = lax.dynamic_index_in_dim(ln_gain, slot_now, 1, keepdims=False)
        down_cols = lax.dynamic_index_in_dim(w_down, slot_now, 1, keepdims=False)
        up_cols = lax.dynamic_index_in_dim(w_up, slot_now, 1, keepdims=False)
        live_rows = row_index < count_now
        token_grad, normed, act_low, grad_inner, masked = adapter_backward(block_x, block_dy, live_rows, gains, down_cols, up_cols)
        part_down = lax.dot_general(normed, grad_inner, (((0,), (0,)), ((), ())), preferred_element_type=jnp.float32)
        part_up = lax.dot_general(masked, act_low, (((0,), (0,)), ((), ())), preferred_element_type=jnp.float32)
        sum_down, sum_up = totals
        start_at = (zero_index, slot_now, zero_index)
        sum_down = lax.dynamic_update_slice(sum_down, lax.dynamic_slice(sum_down, start_at, (D, 1, B)) + part_down[:, None, :], start_at)
        sum_up = lax.dynamic_update_slice(sum_up, lax.dynamic_slice(sum_up, start_at, (D, 1, B)) + part_up[:, None, :], start_at)
        return ((sum_down, sum_up), token_grad)
    start_sums = (jnp.zeros((D, LANGS, B), jnp.float32), jnp.zeros((D, LANGS, B), jnp.float32))
    (sum_down, sum_up), token_grad = lax.scan(one_block, start_sums, (tokens, cotangent, slot_ids, counts))
    scale = 1.0 / BLK
    return (token_grad, (sum_down * scale).astype(jnp.bfloat16), (sum_up * scale).astype(jnp.bfloat16))
```

```python
import functools
import math

import jax
import jax.numpy as jnp
from jax import lax
from jax.experimental import pallas as pl
from jax.experimental.pallas import tpu as pltpu
from jax.sharding import PartitionSpec as P

SLAB = 16
LANES = 128
VMEM_LIMIT = 48 * 1024 * 1024


def pack_kernel(
    dims, lang_ref, count_ref, slot_ref, mp_ref, x_hbm, dy_hbm, out_ref, dest_ref, dy_buf, source_ref, taken_ref, sems
):
    dp_size, capacity, lang_local, full = dims
    block_count, block_rows, features = x_hbm.shape
    slots = dp_size * capacity
    halves = block_rows // SLAB

    def clear_owner(owner, carry):
        taken_ref[owner] = 0
        return carry

    def clear_slot(slot, carry):
        source_ref[slot] = -1
        return carry

    lax.fori_loop(0, dp_size, clear_owner, 0)
    if not full:
        lax.fori_loop(0, slots, clear_slot, 0)

    def place(block, carry):
        owner = slot_ref[lang_ref[block]] // lang_local
        rank = taken_ref[owner]
        taken_ref[owner] = rank + 1
        dest = owner * capacity + rank
        dest_ref[block] = dest
        source_ref[dest] = block
        return carry

    lax.fori_loop(0, block_count, place, 0, unroll=True)

    def copies(slot):
        peer, place_in = slot // capacity, slot % capacity
        block = source_ref[slot]
        block = block if full else jnp.maximum(block, 0)
        result = [pltpu.make_async_copy(dy_hbm.at[block], dy_buf.at[slot], sems.at[0, slot])]
        for half in range(halves):
            group = place_in * halves + half
            result.append(
                pltpu.make_async_copy(
                    x_hbm.at[block, pl.ds(half * SLAB, SLAB)],
                    out_ref.at[peer, :, pl.ds(group * features, features)],
                    sems.at[1 + half, slot],
                )
            )
        return result

    for slot in range(slots):
        if full:
            for copy in copies(slot):
                copy.start()
        else:

            @pl.when(source_ref[slot] >= 0)
            def _():
                for copy in copies(slot):
                    copy.start()

    row_start = mp_ref[0] * block_rows
    dy_groups = capacity * halves
    for slot in range(slots):
        peer, place_in = slot // capacity, slot % capacity

        def finish(slot=slot, peer=peer, place_in=place_in):
            for copy in copies(slot):
                copy.wait()
            block = source_ref[slot]
            live = count_ref[block] - row_start
            for half in range(halves):
                rows = lax.broadcasted_iota(jnp.int32, (SLAB, features), 0) + half * SLAB
                piece = dy_buf[slot, pl.ds(half * SLAB, SLAB), :].astype(jnp.float32)
                group = dy_groups + place_in * halves + half
                out_ref[peer, :, pl.ds(group * features, features)] = jnp.where(rows < live, piece, 0.0).astype(
                    out_ref.dtype
                )

        def blank(peer=peer, place_in=place_in):
            for half in range(halves):
                for base in (0, dy_groups):
                    group = base + place_in * halves + half
                    out_ref[peer, :, pl.ds(group * features, features)] = jnp.zeros((SLAB, features), out_ref.dtype)

        if full:
            finish()
        else:
            pl.when(source_ref[slot] >= 0)(finish)
            pl.when(source_ref[slot] < 0)(blank)

    lane = lax.broadcasted_iota(jnp.int32, (SLAB, LANES), 1)
    for peer in range(dp_size):
        tags = jnp.zeros((SLAB, LANES), jnp.int32)
        for place_in in range(capacity):
            block = source_ref[peer * capacity + place_in]
            safe = block if full else jnp.maximum(block, 0)
            local = slot_ref[lang_ref[safe]] % lang_local
            tags = jnp.where(lane // (LANES // capacity) == place_in, local, tags)
        out_ref[peer, :, pl.ds(2 * dy_groups * features, LANES)] = tags.astype(jnp.float32).astype(out_ref.dtype)


def load_all(dims, mp_ref, recv_hbm, weight_hbms, x_buf, dy_buf, tag_buf, down_buf, up_buf, gain_buf, sems):
    groups, features, shard_rows = dims
    copies = []
    for group in range(groups):
        for base, buf in ((0, x_buf), (groups, dy_buf)):
            copies.append(
                (recv_hbm.at[:, :, pl.ds((base + group) * features, features)], buf.at[:, group])
            )
    copies.append((recv_hbm.at[:, :, pl.ds(2 * groups * features, LANES)], tag_buf))
    for offset, weight in enumerate(weight_hbms):
        rows = pl.ds(pl.multiple_of((mp_ref[0] ^ offset) * shard_rows, shard_rows), shard_rows)
        copies.append((weight.at[pl.ds(0, shard_rows)], down_buf.at[rows]))
        if up_buf is not None:
            copies.append((weight.at[pl.ds(shard_rows, shard_rows)], up_buf.at[rows]))
        copies.append((weight.at[pl.ds(2 * shard_rows, SLAB)], gain_buf.at[offset]))
    started = [pltpu.make_async_copy(src, dst, sems.at[n]) for n, (src, dst) in enumerate(copies)]
    for copy in started:
        copy.start()
    for copy in started:
        copy.wait()


def gain_rows(gain_buf):
    total = gain_buf[0].astype(jnp.float32)
    for offset in range(1, gain_buf.shape[0]):
        total = total + gain_buf[offset].astype(jnp.float32)
    return total[0:1, :], total[1:2, :]


def main_kernel(
    dims,
    mp_ref,
    recv_hbm,
    *refs,
):
    capacity, tile, mp_size, scale = dims
    weight_hbms = refs[:mp_size]
    (tg_ref, send_ref, keep_ref) = refs[mp_size : mp_size + 3]
    (x_buf, dy_buf, tag_buf, down_buf, up_buf, gain_buf, id_buf, normed_buf, act_buf, inner_buf, sems) = refs[
        mp_size + 3 :
    ]
    dp_size, groups, _, features = x_buf.shape
    width = down_buf.shape[1]
    half_width = width // 2
    rows = dp_size * groups * SLAB
    shard = features // mp_size
    load_all(
        (groups, features, shard), mp_ref, recv_hbm, weight_hbms, x_buf, dy_buf, tag_buf, down_buf, up_buf, gain_buf, sems
    )
    per_block = groups // capacity
    for peer in range(dp_size):
        for group in range(groups):
            place_in = group // per_block
            column = place_in * (LANES // capacity)
            tag = tag_buf[peer, :, column : column + 1].astype(jnp.float32)
            start = (peer * groups + group) * SLAB
            id_buf[pl.ds(start, SLAB), :] = jnp.broadcast_to(tag, (SLAB, LANES))
    gain_a, gain_b = gain_rows(gain_buf)
    peers_tile = tile // (groups * SLAB)

    def one_tile(step, carry):
        first = pl.multiple_of(step * tile, tile)
        peers = pl.ds(step * peers_tile, peers_tile)
        values = x_buf[peers].reshape(tile, features).astype(jnp.float32)
        masked = dy_buf[peers].reshape(tile, features)
        tags = id_buf[pl.ds(first, tile), :]
        second = tags[:, :1] > 0.5
        row_mean = jnp.mean(values, axis=-1, keepdims=True)
        centered = values - row_mean
        inv_std = lax.rsqrt(jnp.mean(centered * centered, axis=-1, keepdims=True) + 1e-05)
        unit = centered * inv_std
        gain = jnp.where(second, gain_b, gain_a)
        normed = (unit * gain).astype(jnp.bfloat16)
        normed_buf[pl.ds(first, tile), :] = normed
        inner_both = jnp.dot(normed, down_buf[...], preferred_element_type=jnp.float32)
        inner = jnp.where(second, inner_both[:, half_width:], inner_both[:, :half_width])
        bell = 0.5 * (1.0 + lax.erf(inner * (1.0 / math.sqrt(2.0))))
        act = inner * bell
        slope = bell + inner * jnp.exp(-0.5 * inner * inner) * (1.0 / math.sqrt(2.0 * math.pi))
        grad_act_both = jnp.dot(masked, up_buf[...], preferred_element_type=jnp.float32)
        grad_act = jnp.where(second, grad_act_both[:, half_width:], grad_act_both[:, :half_width])
        grad_inner = grad_act * slope
        act_buf[pl.ds(first, tile), :] = jnp.concatenate(
            [jnp.where(second, 0.0, act), jnp.where(second, act, 0.0)], axis=1
        ).astype(jnp.bfloat16)
        spread = jnp.concatenate(
            [jnp.where(second, 0.0, grad_inner), jnp.where(second, grad_inner, 0.0)], axis=1
        ).astype(jnp.bfloat16)
        inner_buf[pl.ds(first, tile), :] = spread
        grad_normed = lax.dot_general(
            spread, down_buf[...], (((1,), (1,)), ((), ())), preferred_element_type=jnp.float32
        )
        scaled = grad_normed * gain
        token_grad = masked.astype(jnp.float32) + inv_std * (
            scaled
            - jnp.mean(scaled, axis=-1, keepdims=True)
            - unit * jnp.mean(scaled * unit, axis=-1, keepdims=True)
        )
        tg_ref[pl.ds(first, tile), :] = token_grad.astype(jnp.bfloat16)
        return carry

    lax.fori_loop(0, rows // tile, one_tile, 0)

    for offset in range(mp_size):
        lanes = pl.ds(pl.multiple_of((mp_ref[0] ^ offset) * shard, shard), shard)
        out = send_ref if offset % 2 else keep_ref
        masked = dy_buf[:, :, :, lanes].reshape(rows, shard)
        up_part = lax.dot_general(
            masked, act_buf[...], (((0,), (0,)), ((), ())), preferred_element_type=jnp.float32
        )
        out[offset // 2, pl.ds(0, shard), :] = (up_part * scale).astype(jnp.bfloat16)
        down_part = lax.dot_general(
            normed_buf[:, lanes], inner_buf[...], (((0,), (0,)), ((), ())), preferred_element_type=jnp.float32
        )
        out[offset // 2, pl.ds(shard, shard), :] = (down_part * scale).astype(jnp.bfloat16)


def unpack_kernel(dest_ref, back_hbm, out_hbm, sems):
    block_count = out_hbm.shape[0]
    copies = [
        pltpu.make_async_copy(back_hbm.at[dest_ref[block]], out_hbm.at[block], sems.at[block])
        for block in range(block_count)
    ]
    for copy in copies:
        copy.start()
    for copy in copies:
        copy.wait()


def shards(tokens, cotangent, block_lang, counts, slot_of, ln_gain, w_down, w_up):
    block_count, block_rows, features = tokens.shape
    dp_size = lax.axis_size("dp")
    mp_size = lax.axis_size("mp")
    lang_local, bottleneck = w_down.shape[1:]
    shard = w_down.shape[0]
    width = lang_local * bottleneck
    capacity = (block_count + dp_size - 1) // dp_size
    slots = dp_size * capacity
    halves = block_rows // SLAB
    groups = capacity * halves
    packed_lanes = 2 * groups * features + LANES
    mp_index = lax.axis_index("mp").astype(jnp.int32)[None]
    smem = pl.BlockSpec(memory_space=pltpu.SMEM)
    vmem = pl.BlockSpec(memory_space=pltpu.VMEM)
    anywhere = pl.BlockSpec(memory_space=pl.ANY)
    params = pltpu.CompilerParams(vmem_limit_bytes=VMEM_LIMIT)

    send, dest = pl.pallas_call(
        functools.partial(pack_kernel, (dp_size, capacity, lang_local, slots == block_count)),
        out_shape=(
            jax.ShapeDtypeStruct((dp_size, SLAB, packed_lanes), jnp.bfloat16),
            jax.ShapeDtypeStruct((block_count,), jnp.int32),
        ),
        in_specs=[smem, smem, smem, smem, anywhere, anywhere],
        out_specs=(vmem, smem),
        scratch_shapes=[
            pltpu.VMEM((slots, block_rows, features), jnp.bfloat16),
            pltpu.SMEM((slots,), jnp.int32),
            pltpu.SMEM((dp_size,), jnp.int32),
            pltpu.SemaphoreType.DMA((1 + halves, slots)),
        ],
        compiler_params=params,
        name="pack",
    )(block_lang, counts, slot_of, mp_index, tokens, cotangent)
    recv = lax.all_to_all(send, "dp", split_axis=0, concat_axis=0, tiled=True)

    gain_part = lax.dynamic_update_slice(
        jnp.zeros((SLAB, features), jnp.bfloat16), ln_gain.T, (0, mp_index[0] * shard)
    )
    own = jnp.concatenate([w_down.reshape(shard, width), w_up.reshape(shard, width), gain_part], axis=0)

    def swap(array, bit):
        return lax.ppermute(array, "mp", [(i, i ^ bit) for i in range(mp_size)])

    across = swap(own, 2)
    weights = [own, swap(own, 1), across, swap(across, 1)]

    rows = slots * block_rows
    tile = min(128, rows)
    bf = jnp.bfloat16
    token_part, send_grad, keep_grad = pl.pallas_call(
        functools.partial(main_kernel, (capacity, tile, mp_size, 1.0 / (block_rows * mp_size))),
        out_shape=(
            jax.ShapeDtypeStruct((rows, features), bf),
            jax.ShapeDtypeStruct((mp_size // 2, 2 * shard, width), bf),
            jax.ShapeDtypeStruct((mp_size // 2, 2 * shard, width), bf),
        ),
        in_specs=[smem, anywhere] + [anywhere] * mp_size,
        out_specs=(vmem, vmem, vmem),
        scratch_shapes=[
            pltpu.VMEM((dp_size, groups, SLAB, features), bf),
            pltpu.VMEM((dp_size, groups, SLAB, features), bf),
            pltpu.VMEM((dp_size, SLAB, LANES), bf),
            pltpu.VMEM((features, width), bf),
            pltpu.VMEM((features, width), bf),
            pltpu.VMEM((mp_size, SLAB, features), bf),
            pltpu.VMEM((rows, LANES), jnp.float32),
            pltpu.VMEM((rows, features), bf),
            pltpu.VMEM((rows, width), bf),
            pltpu.VMEM((rows, width), bf),
            pltpu.SemaphoreType.DMA((2 * groups + 1 + 3 * mp_size,)),
        ],
        compiler_params=params,
        name="adapter",
    )(mp_index, recv, *weights)

    back = lax.all_to_all(
        token_part.reshape(slots, block_rows, features), "dp", split_axis=0, concat_axis=0, tiled=True
    )
    near = swap(send_grad, 1)
    pair = keep_grad.astype(jnp.float32) + near.astype(jnp.float32)
    far = swap(pair[1].astype(bf), 2)
    total = (pair[0] + far.astype(jnp.float32)).astype(bf)
    grad_up = total[:shard].reshape(shard, lang_local, bottleneck)
    grad_down = total[shard:].reshape(shard, lang_local, bottleneck)
    token_grad = pl.pallas_call(
        unpack_kernel,
        out_shape=jax.ShapeDtypeStruct(tokens.shape, bf),
        in_specs=[smem, anywhere],
        out_specs=anywhere,
        scratch_shapes=[pltpu.SemaphoreType.DMA((block_count,))],
        name="unpack",
    )(dest, back)
    return (token_grad, grad_down, grad_up)


def solution(mesh):
    placed = (
        P("dp", "mp", None),
        P("dp", "mp", None),
        P("dp"),
        P("dp"),
        P(),
        P("mp", "dp"),
        P("mp", "dp", None),
        P("mp", "dp", None),
    )
    return jax.shard_map(
        shards,
        mesh=mesh,
        in_specs=placed,
        out_specs=(P("dp", "mp", None), P("mp", "dp", None), P("mp", "dp", None)),
        check_vma=False,
    )
```

```python
import functools
import math

import jax
import jax.numpy as jnp
from jax import lax
from jax.experimental import pallas as pl
from jax.experimental.pallas import tpu as pltpu
from jax.sharding import PartitionSpec as P

SLAB = 16
LANES = 128
MIB = 1024 * 1024
ANYWHERE = pl.BlockSpec(memory_space=pl.ANY)
VMEM = pl.BlockSpec(memory_space=pltpu.VMEM)
SMEM = pl.BlockSpec(memory_space=pltpu.SMEM)


def params(mib):
    return pltpu.CompilerParams(vmem_limit_bytes=min(mib, 60) * MIB)


def start_all(copies):
    for copy in copies:
        copy.start()


def wait_all(copies):
    for copy in copies:
        copy.wait()


def payload_kernel(after_ref, down_ref, up_ref, gain_ref, out_ref):
    shard = down_ref.shape[0]
    for n, ref in enumerate((down_ref, up_ref)):
        values = ref[...]
        out_ref[pl.ds(n * shard, shard), :] = jnp.concatenate(
            [values[:, local, :] for local in range(values.shape[1])], axis=1
        )
    tail = pl.ds(2 * shard, SLAB)
    out_ref[tail, :] = jnp.zeros((SLAB, out_ref.shape[1]), out_ref.dtype)
    lanes = pl.ds(pl.multiple_of(lax.axis_index("mp") * shard, shard), shard)
    gains = gain_ref[...].astype(jnp.float32)
    rows = [gains, jnp.zeros((SLAB - gains.shape[0], shard), jnp.float32)]
    out_ref[tail, lanes] = jnp.concatenate(rows, axis=0).astype(out_ref.dtype)


def pack_kernel(dims, lang_hbm, count_hbm, slot_hbm, x_hbm, dy_hbm, out_hbm, source_ref, *scratch):
    dp_size, capacity, lang_local, full = dims
    block_count, block_rows, features = x_hbm.shape
    slots = dp_size * capacity
    halves = block_rows // SLAB
    packed, x_buf, dy_buf, lang_ref, count_ref, slot_ref, taken_ref, sems, out_sems = scratch
    loads = [
        pltpu.make_async_copy(src, dst, sems.at[n])
        for n, (src, dst) in enumerate(
            (
                (lang_hbm, lang_ref),
                (count_hbm, count_ref),
                (slot_hbm, slot_ref),
                (x_hbm, x_buf),
                (dy_hbm, dy_buf),
            )
        )
    ]
    start_all(loads)

    def clear_owner(owner, carry):
        taken_ref[owner] = 0
        return carry

    def clear_slot(slot, carry):
        source_ref[slot] = -1
        return carry

    lax.fori_loop(0, dp_size, clear_owner, 0, unroll=dp_size <= 8)
    if not full:
        lax.fori_loop(0, slots, clear_slot, 0)
    wait_all(loads[:3])

    def place(block, carry):
        owner = slot_ref[lang_ref[block]] // lang_local
        rank = taken_ref[owner]
        taken_ref[owner] = rank + 1
        source_ref[owner * capacity + rank] = block
        return carry

    lax.fori_loop(0, block_count, place, 0, unroll=True)
    wait_all(loads[3:])
    row_start = lax.axis_index("mp") * block_rows
    dy_groups = capacity * halves
    lane = lax.broadcasted_iota(jnp.int32, (SLAB, LANES), 1)

    def lanes_of(group):
        return pl.ds(group * features, features)

    def fill(peer, place_in):
        block = source_ref[peer * capacity + place_in]
        live = count_ref[block] - row_start
        for half in range(halves):
            here = pl.ds(half * SLAB, SLAB)
            group = place_in * halves + half
            packed[peer, :, lanes_of(group)] = x_buf[block, here, :]
            rows = lax.broadcasted_iota(jnp.int32, (SLAB, features), 0) + half * SLAB
            piece = dy_buf[block, here, :].astype(jnp.float32)
            packed[peer, :, lanes_of(dy_groups + group)] = jnp.where(rows < live, piece, 0.0).astype(jnp.bfloat16)

    def blank(peer, place_in):
        for half in range(halves):
            for base in (0, dy_groups):
                group = base + place_in * halves + half
                packed[peer, :, lanes_of(group)] = jnp.zeros((SLAB, features), jnp.bfloat16)

    def one_peer(peer, carry):
        tags = jnp.zeros((SLAB, LANES), jnp.int32)
        for place_in in range(capacity):
            block = source_ref[peer * capacity + place_in]
            if full:
                fill(peer, place_in)
            else:
                pl.when(block >= 0)(functools.partial(fill, peer, place_in))
                pl.when(block < 0)(functools.partial(blank, peer, place_in))
                block = jnp.maximum(block, 0)
            local = slot_ref[lang_ref[block]] % lang_local
            tags = jnp.where(lane // (LANES // capacity) == place_in, local, tags)
        packed[peer, :, pl.ds(2 * dy_groups * features, LANES)] = tags.astype(jnp.float32).astype(jnp.bfloat16)
        pltpu.make_async_copy(packed.at[peer], out_hbm.at[peer], out_sems.at[peer]).start()
        return carry

    def wait_peer(peer, carry):
        pltpu.make_async_copy(packed.at[peer], out_hbm.at[peer], out_sems.at[peer]).wait()
        return carry

    lax.fori_loop(0, dp_size, one_peer, 0, unroll=dp_size <= 8)
    lax.fori_loop(0, dp_size, wait_peer, 0, unroll=dp_size <= 8)


def spread(values, second):
    return jnp.concatenate([jnp.where(second, 0.0, values), jnp.where(second, values, 0.0)], axis=1).astype(jnp.bfloat16)


def pick(values, second):
    half = values.shape[1] // 2
    return jnp.where(second, values[:, half:], values[:, :half])


def wide(column):
    return jnp.broadcast_to(column, (column.shape[0], LANES))


def gains_of(gain_ref, second):
    return jnp.where(second, gain_ref[1:2, :], gain_ref[0:1, :])


def normalize(values, second, gain_ref):
    values = values.astype(jnp.float32)
    row_mean = jnp.mean(values, axis=-1, keepdims=True)
    centered = values - row_mean
    inv_std = lax.rsqrt(jnp.mean(centered * centered, axis=-1, keepdims=True) + 1e-05)
    normed = (centered * inv_std * gains_of(gain_ref, second)).astype(jnp.bfloat16)
    return row_mean, inv_std, normed


def middle(masked, inner, second, up_ref):
    bell = 0.5 * (1.0 + lax.erf(inner * (1.0 / math.sqrt(2.0))))
    slope = bell + inner * jnp.exp(-0.5 * inner * inner) * (1.0 / math.sqrt(2.0 * math.pi))
    grad_act = pick(jnp.dot(masked, up_ref[...], preferred_element_type=jnp.float32), second)
    return spread(inner * bell, second), spread(grad_act * slope, second)


def backward(values, masked, row_mean, inv_std, second, grad_inner, gain_ref, down_ref):
    grad_normed = lax.dot_general(
        grad_inner, down_ref[...], (((1,), (1,)), ((), ())), preferred_element_type=jnp.float32
    )
    unit = (values.astype(jnp.float32) - row_mean) * inv_std
    scaled = grad_normed * gains_of(gain_ref, second)
    token_grad = masked.astype(jnp.float32) + inv_std * (
        scaled - jnp.mean(scaled, axis=-1, keepdims=True) - unit * jnp.mean(scaled * unit, axis=-1, keepdims=True)
    )
    return token_grad.astype(jnp.bfloat16)


def weight_grad_kernel(dims, recv_hbm, own_hbm, across_hbm, both_hbm, *refs):
    capacity, mp_size, tile, scale = dims
    part_refs, (x_buf, dy_buf, inner_buf, stats_buf, id_buf, down_ref, gain_ref) = refs[:4], refs[4:11]
    raw, up_ref, gain_buf, normed_buf, act_buf, sems, weight_sems = refs[11:]
    chunks, _, lanes = raw.shape
    rows, features = x_buf.shape
    groups = rows // (chunks * SLAB)
    shard = features // mp_size
    size = own_hbm.shape[0]
    split = groups * features

    def recv_copy(n, start, count):
        return pltpu.make_async_copy(
            recv_hbm.at[:, :, pl.ds(start, count)], raw.at[:, :, pl.ds(start, count)], sems.at[n]
        )

    first = [recv_copy(0, 0, split), recv_copy(1, 2 * split, LANES)]
    then, later = [], [recv_copy(2, split, split)]
    for offset, weight in enumerate(
        (own_hbm, both_hbm.at[pl.ds(0, size)], across_hbm, both_hbm.at[pl.ds(size, size)])
    ):
        here = pl.ds(pl.multiple_of((lax.axis_index("mp") ^ offset) * shard, shard), shard)
        for n, (group, src, dst) in enumerate(
            (
                (then, weight.at[pl.ds(0, shard)], down_ref.at[here]),
                (first, weight.at[pl.ds(2 * shard, SLAB)], gain_buf.at[offset]),
                (later, weight.at[pl.ds(shard, shard)], up_ref.at[here]),
            )
        ):
            group.append(pltpu.make_async_copy(src, dst, weight_sems.at[n, offset]))
    start_all(first)
    start_all(then)
    start_all(later)
    wait_all(first)
    gain = gain_buf[0].astype(jnp.float32)
    for offset in range(1, mp_size):
        gain = gain + gain_buf[offset].astype(jnp.float32)
    gain_ref[...] = gain
    tile_chunks = tile // (groups * SLAB)
    per_block = groups // capacity

    def rows_of(step, base):
        return jnp.concatenate(
            [
                raw[step * tile_chunks + chunk, :, pl.ds((base + group) * features, features)]
                for chunk in range(tile_chunks)
                for group in range(groups)
            ],
            axis=0,
        )

    def ids_of(step):
        pieces = []
        for chunk in range(tile_chunks):
            tags = raw[step * tile_chunks + chunk, :, pl.ds(2 * split, LANES)].astype(jnp.float32)
            for group in range(groups):
                column = (group // per_block) * (LANES // capacity)
                pieces.append(wide(tags[:, column : column + 1]))
        return jnp.concatenate(pieces, axis=0)

    whole = rows == tile
    if not whole:
        wait_all(then + later)

    def one_tile(step, carry):
        here = pl.ds(pl.multiple_of(step * tile, tile), tile)
        ids = ids_of(step)
        id_buf[here, :] = ids
        second = ids[:, :1] > 0.5
        values = rows_of(step, 0)
        x_buf[here, :] = values
        row_mean, inv_std, normed = normalize(values, second, gain_ref)
        normed_buf[here, :] = normed
        stats_buf[here, :] = jnp.concatenate([wide(row_mean), wide(inv_std)], axis=1)
        if whole:
            wait_all(then)
        inner = pick(jnp.dot(normed_buf[here, :], down_ref[...], preferred_element_type=jnp.float32), second)
        if whole:
            wait_all(later)
        dy_buf[here, :] = rows_of(step, groups)
        act, grad_inner = middle(dy_buf[here, :], inner, second, up_ref)
        act_buf[here, :] = act
        inner_buf[here, :] = grad_inner
        return carry

    if whole:
        one_tile(0, 0)
    else:
        lax.fori_loop(0, rows // tile, one_tile, 0)
    for kind, (left, right) in enumerate(((dy_buf, act_buf), (normed_buf, inner_buf))):
        for offset in range(mp_size):
            here = pl.ds(pl.multiple_of((lax.axis_index("mp") ^ offset) * shard, shard), shard)
            part = lax.dot_general(
                left[:, here], right[...], (((0,), (0,)), ((), ())), preferred_element_type=jnp.float32
            )
            part_refs[2 * kind + offset % 2][offset // 2] = (part * scale).astype(jnp.bfloat16)


def token_grad_kernel(tile, x_ref, dy_ref, inner_ref, stats_ref, id_ref, down_ref, gain_ref, out_hbm, grad_buf, sems):
    steps = grad_buf.shape[0] // tile

    def copy(step):
        here = pl.ds(pl.multiple_of(step * tile, tile), tile)
        return pltpu.make_async_copy(grad_buf.at[here], out_hbm.at[here], sems.at[step])

    def one_tile(step, carry):
        here = pl.ds(pl.multiple_of(step * tile, tile), tile)
        stats = stats_ref[here, :]
        grad_buf[here, :] = backward(
            x_ref[here, :],
            dy_ref[here, :],
            stats[:, :1],
            stats[:, LANES : LANES + 1],
            id_ref[here, :][:, :1] > 0.5,
            inner_ref[here, :],
            gain_ref,
            down_ref,
        )
        copy(step).start()
        return carry

    def finish(step, carry):
        copy(step).wait()
        return carry

    lax.fori_loop(0, steps, one_tile, 0, unroll=steps <= 2)
    lax.fori_loop(0, steps, finish, 0, unroll=steps <= 2)


def add_kernel(keep_ref, near_ref, *refs):
    out_ref = refs[-1]
    total = keep_ref[1].astype(jnp.float32) + near_ref[1].astype(jnp.float32)
    out_ref[...] = total.astype(out_ref.dtype)


def finish_grad(keep_ref, near_ref, far_ref, out_ref):
    total = keep_ref[0].astype(jnp.float32) + near_ref[0].astype(jnp.float32) + far_ref[...].astype(jnp.float32)
    out_ref[...] = total.reshape(out_ref.shape).astype(out_ref.dtype)


def tail_kernel(full, source_ref, back_hbm, keep_hbm, near_hbm, far_hbm, out_hbm, grad_ref, buf, *scratch):
    sums, (sum_sems, in_sems, out_sems) = scratch[:3], scratch[3:]
    slots = back_hbm.shape[0]
    terms = [
        pltpu.make_async_copy(src, dst, sum_sems.at[n])
        for n, (src, dst) in enumerate(zip((keep_hbm.at[0], near_hbm.at[0], far_hbm), sums))
    ]

    def load(slot):
        return pltpu.make_async_copy(back_hbm.at[slot], buf.at[slot], in_sems.at[slot])

    def store(slot, do):
        block = source_ref[slot]
        copy = pltpu.make_async_copy(
            buf.at[slot], out_hbm.at[block if full else jnp.maximum(block, 0)], out_sems.at[slot]
        )
        if full:
            getattr(copy, do)()
        else:
            pl.when(block >= 0)(getattr(copy, do))

    start_all([load(slot) for slot in range(slots)])
    start_all(terms)
    for slot in range(slots):
        load(slot).wait()
        store(slot, "start")
    wait_all(terms)
    total = sums[0][...].astype(jnp.float32) + sums[1][...].astype(jnp.float32) + sums[2][...].astype(jnp.float32)
    grad_ref[...] = total.reshape(grad_ref.shape).astype(grad_ref.dtype)
    for slot in range(slots):
        store(slot, "wait")


def shards(tokens, cotangent, block_lang, counts, slot_of, ln_gain, w_down, w_up):
    block_count, block_rows, features = tokens.shape
    dp_size = lax.axis_size("dp")
    mp_size = lax.axis_size("mp")
    lang_local, bottleneck = w_down.shape[1:]
    shard = w_down.shape[0]
    width = lang_local * bottleneck
    capacity = (block_count + dp_size - 1) // dp_size
    slots = dp_size * capacity
    full = slots == block_count
    halves = block_rows // SLAB
    groups = capacity * halves
    lanes = 2 * groups * features + LANES
    rows = slots * block_rows
    tile = min(512, rows)
    resident = rows <= tile
    bf = jnp.bfloat16

    def shape(*extent, kind=bf):
        return jax.ShapeDtypeStruct(extent, kind)

    def vmem_shape(*extent, kind=bf):
        return pltpu.VMEM(extent, kind) if resident else shape(*extent, kind=kind)

    def in_vmem(*arrays):
        return [pltpu.with_memory_space_constraint(array, pltpu.VMEM) if resident else array for array in arrays]

    def in_hbm(*arrays):
        return [pltpu.with_memory_space_constraint(array, pltpu.HBM) for array in arrays]

    def swap(array, bit):
        return lax.ppermute(array, "mp", [(i, i ^ bit) for i in range(mp_size)])

    def exchange(array):
        return lax.all_to_all(array, "dp", split_axis=0, concat_axis=0, tiled=True)

    packed, source = pl.pallas_call(
        functools.partial(pack_kernel, (dp_size, capacity, lang_local, full)),
        out_shape=(pltpu.HBM((dp_size, SLAB, lanes), bf), shape(slots, kind=jnp.int32)),
        in_specs=[ANYWHERE] * 5,
        out_specs=(ANYWHERE, SMEM),
        scratch_shapes=[
            pltpu.VMEM((dp_size, SLAB, lanes), bf),
            pltpu.VMEM(tokens.shape, bf),
            pltpu.VMEM(cotangent.shape, bf),
            pltpu.SMEM(block_lang.shape, jnp.int32),
            pltpu.SMEM(counts.shape, jnp.int32),
            pltpu.SMEM(slot_of.shape, jnp.int32),
            pltpu.SMEM((dp_size,), jnp.int32),
            pltpu.SemaphoreType.DMA((5,)),
            pltpu.SemaphoreType.DMA((dp_size,)),
        ],
        compiler_params=params(8 + slots // 4),
        name="pack",
    )(*in_hbm(block_lang, counts, slot_of, tokens, cotangent))
    recv = exchange(packed)

    own = pl.pallas_call(
        payload_kernel,
        out_shape=shape(2 * shard + SLAB, width),
        in_specs=[SMEM] + [VMEM] * 3,
        out_specs=VMEM,
        compiler_params=params(8),
        name="payload",
    )(source, w_down, w_up, ln_gain.T)
    across = swap(own, 2)
    both = swap(jnp.concatenate([own, across], axis=0), 1)
    part = vmem_shape(mp_size // 2, shard, width)
    up_keep, up_send, down_keep, down_send, *kept = pl.pallas_call(
        functools.partial(weight_grad_kernel, (capacity, mp_size, tile, 1.0 / (block_rows * mp_size))),
        out_shape=(
            part,
            part,
            part,
            part,
            vmem_shape(rows, features),
            vmem_shape(rows, features),
            vmem_shape(rows, width),
            vmem_shape(rows, 2 * LANES, kind=jnp.float32),
            vmem_shape(rows, LANES, kind=jnp.float32),
            vmem_shape(features, width),
            vmem_shape(SLAB, features, kind=jnp.float32),
        ),
        in_specs=[ANYWHERE] * 4,
        out_specs=(VMEM,) * 11,
        scratch_shapes=[
            pltpu.VMEM((dp_size, SLAB, lanes), bf),
            pltpu.VMEM((features, width), bf),
            pltpu.VMEM((mp_size, SLAB, features), bf),
            pltpu.VMEM((rows, features), bf),
            pltpu.VMEM((rows, width), bf),
            pltpu.SemaphoreType.DMA((3,)),
            pltpu.SemaphoreType.DMA((3, mp_size)),
        ],
        compiler_params=params(14 + rows // 48),
        name="weight_grads",
    )(*in_hbm(recv, own, across, both))

    tile = min(256, rows)
    token_part = pl.pallas_call(
        functools.partial(token_grad_kernel, tile),
        out_shape=pltpu.HBM((rows, features), bf),
        in_specs=[VMEM] * 7,
        out_specs=ANYWHERE,
        scratch_shapes=[pltpu.VMEM((rows, features), bf), pltpu.SemaphoreType.DMA((rows // tile,))],
        compiler_params=params(4 + rows // 64),
        name="token_grads",
    )(*in_vmem(*kept))

    def reduce_core(keep, send, name, *through):
        near = swap(send, 1)
        *through, partial_sum = pl.pallas_call(
            add_kernel,
            out_shape=(*[pltpu.HBM(array.shape, array.dtype) for array in through], vmem_shape(shard, width)),
            in_specs=[VMEM] * 2 + [ANYWHERE] * len(through),
            out_specs=(*[ANYWHERE] * len(through), VMEM),
            input_output_aliases={2 + n: n for n in range(len(through))},
            compiler_params=params(4),
            name=name + "_add",
        )(*in_vmem(keep, near), *in_hbm(*through))
        return near, partial_sum, *through

    up_near, up_sum, token_part = reduce_core(up_keep, up_send, "up", token_part)
    down_near, down_sum = reduce_core(down_keep, down_send, "down")
    up_far, down_far = swap(up_sum, 2), swap(down_sum, 2)
    back = exchange(token_part.reshape(slots, block_rows, features))
    grad_shape = shape(shard, lang_local, bottleneck)
    grad_up = pl.pallas_call(
        finish_grad,
        out_shape=grad_shape,
        in_specs=[VMEM] * 3,
        out_specs=VMEM,
        compiler_params=params(8),
        name="up_finish",
    )(*in_hbm(up_keep, up_near, up_far))
    token_grad, grad_down = pl.pallas_call(
        functools.partial(tail_kernel, full),
        out_shape=(shape(*tokens.shape), grad_shape),
        in_specs=[SMEM] + [ANYWHERE] * 4,
        out_specs=(ANYWHERE, VMEM),
        scratch_shapes=[
            pltpu.VMEM((slots, block_rows, features), bf),
            pltpu.VMEM((shard, width), bf),
            pltpu.VMEM((shard, width), bf),
            pltpu.VMEM((shard, width), bf),
            pltpu.SemaphoreType.DMA((3,)),
            pltpu.SemaphoreType.DMA((slots,)),
            pltpu.SemaphoreType.DMA((slots,)),
        ],
        compiler_params=params(8 + slots // 8),
        name="tail",
    )(source, *in_hbm(back, down_keep, down_near, down_far))
    return (token_grad, grad_down, grad_up)


def solution(mesh):
    placed = (
        P("dp", "mp", None),
        P("dp", "mp", None),
        P("dp"),
        P("dp"),
        P(),
        P("mp", "dp"),
        P("mp", "dp", None),
        P("mp", "dp", None),
    )
    return jax.shard_map(
        shards,
        mesh=mesh,
        in_specs=placed,
        out_specs=(P("dp", "mp", None), P("mp", "dp", None), P("mp", "dp", None)),
        check_vma=False,
    )
```

```python
import functools
import math

import jax
import jax.numpy as jnp
from jax import lax
from jax.experimental import pallas as pl
from jax.experimental.pallas import tpu as pltpu
from jax.sharding import PartitionSpec as P

SLAB = 16
LANES = 128
MIB = 1024 * 1024
OFFSETS = (0, 4, 1, 5, 2, 6, 3, 7)
ANYWHERE = pl.BlockSpec(memory_space=pl.ANY)
VMEM = pl.BlockSpec(memory_space=pltpu.VMEM)
SMEM = pl.BlockSpec(memory_space=pltpu.SMEM)


def params(mib):
    return pltpu.CompilerParams(vmem_limit_bytes=min(mib, 60) * MIB)


def start_all(copies):
    for copy in copies:
        copy.start()


def wait_all(copies):
    for copy in copies:
        copy.wait()


def pair_kernel(after_ref, own_hbm, core_hbm, out_ref, sems):
    size = own_hbm.shape[0]
    copies = [
        pltpu.make_async_copy(src, out_ref.at[pl.ds(n * size, size)], sems.at[n])
        for n, src in enumerate((own_hbm, core_hbm))
    ]
    start_all(copies)
    wait_all(copies)


def pack_kernel(dims, lang_hbm, count_hbm, slot_hbm, x_hbm, dy_hbm, *refs):
    dp_size, capacity, lang_local, full, direct = dims
    chunks, (source_ref, *scratch) = (refs[:dp_size], refs[dp_size:]) if direct else (None, refs[1:])
    block_count, block_rows, features = x_hbm.shape
    slots = dp_size * capacity
    halves = block_rows // SLAB
    x_buf, dy_buf, lang_ref, count_ref, slot_ref, taken_ref, sems, *scratch = scratch
    if not direct:
        out_hbm, (packed, out_sem) = refs[0], scratch
    loads = [
        pltpu.make_async_copy(src, dst, sems.at[n])
        for n, (src, dst) in enumerate(
            (
                (lang_hbm, lang_ref),
                (count_hbm, count_ref),
                (slot_hbm, slot_ref),
                (x_hbm, x_buf),
                (dy_hbm, dy_buf),
            )
        )
    ]
    start_all(loads)

    def clear_owner(owner, carry):
        taken_ref[owner] = 0
        return carry

    def clear_slot(slot, carry):
        source_ref[slot] = -1
        return carry

    lax.fori_loop(0, dp_size, clear_owner, 0, unroll=dp_size <= 8)
    if not full:
        lax.fori_loop(0, slots, clear_slot, 0)
    wait_all(loads[:3])

    def place(block, carry):
        owner = slot_ref[lang_ref[block]] // lang_local
        rank = taken_ref[owner]
        taken_ref[owner] = rank + 1
        source_ref[owner * capacity + rank] = block
        return carry

    lax.fori_loop(0, block_count, place, 0, unroll=True)
    wait_all(loads[3:])
    row_start = lax.axis_index("mp") * block_rows
    dy_groups = capacity * halves
    lane = lax.broadcasted_iota(jnp.int32, (SLAB, LANES), 1)

    def lanes_of(group):
        return pl.ds(group * features, features)

    def fill(out, block, place_in):
        live = count_ref[block] - row_start
        for half in range(halves):
            here = pl.ds(half * SLAB, SLAB)
            group = place_in * halves + half
            out[:, lanes_of(group)] = x_buf[block, here, :]
            rows = lax.broadcasted_iota(jnp.int32, (SLAB, features), 0) + half * SLAB
            piece = dy_buf[block, here, :].astype(jnp.float32)
            out[:, lanes_of(dy_groups + group)] = jnp.where(rows < live, piece, 0.0).astype(jnp.bfloat16)

    def blank(out, place_in):
        for half in range(halves):
            for base in (0, dy_groups):
                group = base + place_in * halves + half
                out[:, lanes_of(group)] = jnp.zeros((SLAB, features), jnp.bfloat16)

    def one_peer(out, peer):
        tags = jnp.zeros((SLAB, LANES), jnp.int32)
        for place_in in range(capacity):
            block = source_ref[peer * capacity + place_in]
            if full:
                fill(out, block, place_in)
            else:
                pl.when(block >= 0)(functools.partial(fill, out, block, place_in))
                pl.when(block < 0)(functools.partial(blank, out, place_in))
                block = jnp.maximum(block, 0)
            local = slot_ref[lang_ref[block]] % lang_local
            tags = jnp.where(lane // (LANES // capacity) == place_in, local, tags)
        out[:, pl.ds(2 * dy_groups * features, LANES)] = tags.astype(jnp.float32).astype(jnp.bfloat16)

    if direct:
        for offset, out in zip(direct, chunks):
            one_peer(out, lax.axis_index("dp") ^ offset)
    else:

        def send_peer(peer, carry):
            one_peer(packed.at[peer], peer)
            pltpu.make_async_copy(packed.at[peer], out_hbm.at[peer], out_sem).start()
            return carry

        lax.fori_loop(0, dp_size, send_peer, 0)
        pltpu.make_async_copy(packed, out_hbm, out_sem).wait()


def spread(values, second):
    return jnp.concatenate([jnp.where(second, 0.0, values), jnp.where(second, values, 0.0)], axis=1).astype(jnp.bfloat16)


def pick(values, second):
    half = values.shape[1] // 2
    return jnp.where(second, values[:, half:], values[:, :half])


def wide(column):
    return jnp.broadcast_to(column, (column.shape[0], LANES))


def gains_of(gain_ref, second):
    return jnp.where(second, gain_ref[1:2, :], gain_ref[0:1, :])


def normalize(values, second, gain_ref):
    values = values.astype(jnp.float32)
    row_mean = jnp.mean(values, axis=-1, keepdims=True)
    centered = values - row_mean
    inv_std = lax.rsqrt(jnp.mean(centered * centered, axis=-1, keepdims=True) + 1e-05)
    normed = (centered * inv_std * gains_of(gain_ref, second)).astype(jnp.bfloat16)
    return row_mean, inv_std, normed


def middle(masked, inner, second, up_ref):
    bell = 0.5 * (1.0 + lax.erf(inner * (1.0 / math.sqrt(2.0))))
    slope = bell + inner * jnp.exp(-0.5 * inner * inner) * (1.0 / math.sqrt(2.0 * math.pi))
    grad_act = pick(jnp.dot(masked, up_ref[...], preferred_element_type=jnp.float32), second)
    return spread(inner * bell, second), spread(grad_act * slope, second)


def backward(values, masked, row_mean, inv_std, second, grad_inner, gain_ref, down_ref):
    grad_normed = lax.dot_general(
        grad_inner, down_ref[...], (((1,), (1,)), ((), ())), preferred_element_type=jnp.float32
    )
    unit = (values.astype(jnp.float32) - row_mean) * inv_std
    scaled = grad_normed * gains_of(gain_ref, second)
    token_grad = masked.astype(jnp.float32) + inv_std * (
        scaled - jnp.mean(scaled, axis=-1, keepdims=True) - unit * jnp.mean(scaled * unit, axis=-1, keepdims=True)
    )
    return token_grad.astype(jnp.bfloat16)


def weight_grad_kernel(dims, *refs):
    capacity, mp_size, tile, scale, direct = dims
    source_count = len(direct) or 1
    sources, (pair_hbm, far_hbm), refs = refs[:source_count], refs[source_count:][:2], refs[source_count + 2 :]
    part_refs, (x_buf, dy_buf, inner_buf, stats_buf, id_buf, down_ref, gain_ref) = refs[:4], refs[4:11]
    up_ref, gain_buf, normed_buf, act_buf, sems, weight_sems, *scratch = refs[11:]
    rows, features = x_buf.shape
    shard = features // mp_size
    first, then, later = [], [], []
    if direct:
        raw = sources
        chunks = len(direct)
    else:
        (raw,) = scratch
        chunks = raw.shape[0]
    groups = rows // (chunks * SLAB)
    split = groups * features
    if not direct:
        first.append(pltpu.make_async_copy(sources[0], raw, sems))
    size = pair_hbm.shape[0] // 2
    for offset in range(mp_size):
        weight, start = (pair_hbm, far_hbm)[offset // 2], offset % 2 * size
        here = pl.ds(pl.multiple_of((lax.axis_index("mp") ^ offset) * shard, shard), shard)
        for n, (group, src, dst) in enumerate(
            (
                (first, weight.at[pl.ds(start + 2 * shard, SLAB)], gain_buf.at[offset]),
                (then, weight.at[pl.ds(start, shard)], down_ref.at[here]),
                (later, weight.at[pl.ds(start + shard, shard)], up_ref.at[here]),
            )
        ):
            group.append(pltpu.make_async_copy(src, dst, weight_sems.at[n, offset]))
    start_all(first)
    start_all(then)
    start_all(later)
    wait_all(first)
    gain = gain_buf[0].astype(jnp.float32)
    for offset in range(1, mp_size):
        gain = gain + gain_buf[offset].astype(jnp.float32)
    gain_ref[...] = gain
    tile_chunks = tile // (groups * SLAB)
    per_block = groups // capacity

    def chunk_of(step, chunk):
        return raw[chunk] if direct else raw.at[step * tile_chunks + chunk]

    def rows_of(step, base):
        return jnp.concatenate(
            [
                chunk_of(step, chunk)[:, pl.ds((base + group) * features, features)]
                for chunk in range(tile_chunks)
                for group in range(groups)
            ],
            axis=0,
        )

    def ids_of(step):
        pieces = []
        for chunk in range(tile_chunks):
            tags = chunk_of(step, chunk)[:, pl.ds(2 * split, LANES)].astype(jnp.float32)
            for group in range(groups):
                column = (group // per_block) * (LANES // capacity)
                pieces.append(wide(tags[:, column : column + 1]))
        return jnp.concatenate(pieces, axis=0)

    whole = rows == tile
    if not whole:
        wait_all(then + later)

    def one_tile(step, carry):
        here = pl.ds(pl.multiple_of(step * tile, tile), tile)
        ids = ids_of(step)
        id_buf[here, :] = ids
        second = ids[:, :1] > 0.5
        values = rows_of(step, 0)
        x_buf[here, :] = values
        row_mean, inv_std, normed = normalize(values, second, gain_ref)
        normed_buf[here, :] = normed
        stats_buf[here, :] = jnp.concatenate([wide(row_mean), wide(inv_std)], axis=1)
        if whole:
            wait_all(then)
        inner = pick(jnp.dot(normed_buf[here, :], down_ref[...], preferred_element_type=jnp.float32), second)
        if whole:
            wait_all(later)
        dy_buf[here, :] = rows_of(step, groups)
        act, grad_inner = middle(dy_buf[here, :], inner, second, up_ref)
        act_buf[here, :] = act
        inner_buf[here, :] = grad_inner
        return carry

    if whole:
        one_tile(0, 0)
    else:
        lax.fori_loop(0, rows // tile, one_tile, 0)
    for kind, (left, right) in enumerate(((dy_buf, act_buf), (normed_buf, inner_buf))):
        for offset in range(mp_size):
            here = pl.ds(pl.multiple_of((lax.axis_index("mp") ^ offset) * shard, shard), shard)
            part = lax.dot_general(
                left[:, here], right[...], (((0,), (0,)), ((), ())), preferred_element_type=jnp.float32
            )
            part_refs[2 * kind + offset % 2][offset // 2] = (part * scale).astype(jnp.bfloat16)


def token_grad_kernel(tile, chunk_rows, direct, x_ref, dy_ref, inner_ref, stats_ref, id_ref, down_ref, gain_ref, *refs):
    rows = x_ref.shape[0]

    def part(here):
        stats = stats_ref[here, :]
        return backward(
            x_ref[here, :],
            dy_ref[here, :],
            stats[:, :1],
            stats[:, LANES : LANES + 1],
            id_ref[here, :][:, :1] > 0.5,
            inner_ref[here, :],
            gain_ref,
            down_ref,
        )

    if direct:
        for step in range(rows // tile):
            token_grad = part(pl.ds(step * tile, tile))
            for n in range(tile // chunk_rows):
                refs[step * (tile // chunk_rows) + n][...] = token_grad[n * chunk_rows : (n + 1) * chunk_rows]
        return
    out_hbm, grad_buf, sem = refs

    def one_tile(step, carry):
        here = pl.ds(pl.multiple_of(step * tile, tile), tile)
        grad_buf[here, :] = part(here)
        pltpu.make_async_copy(grad_buf.at[here], out_hbm.at[here], sem).start()
        return carry

    lax.fori_loop(0, rows // tile, one_tile, 0)
    pltpu.make_async_copy(grad_buf, out_hbm, sem).wait()


def up_add_kernel(keep_ref, near_ref, *refs):
    sum_ref = refs[-1]
    sum_ref[...] = (keep_ref[1].astype(jnp.float32) + near_ref[1].astype(jnp.float32)).astype(sum_ref.dtype)


def down_add_kernel(keep_ref, near_ref, sum_ref, own_ref):
    total = keep_ref[...].astype(jnp.float32) + near_ref[...].astype(jnp.float32)
    sum_ref[...] = total[1].reshape(sum_ref.shape).astype(sum_ref.dtype)
    own_ref[...] = total[0].reshape(own_ref.shape)


def finish_grad(keep_ref, near_ref, far_ref, out_ref):
    total = keep_ref[0].astype(jnp.float32) + near_ref[0].astype(jnp.float32) + far_ref[...].astype(jnp.float32)
    out_ref[...] = total.reshape(out_ref.shape).astype(out_ref.dtype)


def tail_kernel(dims, source_ref, own_hbm, far_ref, *refs):
    capacity, full, direct = dims
    back_count = len(direct) or 1
    backs, (out_hbm, grad_hbm, own, grad, sems, out_sems, *buf) = refs[:back_count], refs[back_count:]
    slots = out_sems.shape[0]
    block_rows = out_hbm.shape[1]
    half = slots // 2
    term = pltpu.make_async_copy(own_hbm, own, sems.at[0])
    term.start()

    def store(slot, piece):
        if full:
            return pltpu.make_async_copy(piece, out_hbm.at[source_ref[slot]], out_sems.at[0])
        return pltpu.make_async_copy(piece, out_hbm.at[jnp.maximum(source_ref[slot], 0)], out_sems.at[slot])

    if direct:
        for offset, back in zip(direct, backs):
            for place_in in range(capacity):
                slot = (lax.axis_index("dp") ^ offset) * capacity + place_in
                store(slot, back.at[pl.ds(place_in * block_rows, block_rows)]).start()
    else:
        (buf,) = buf
        loads = [
            pltpu.make_async_copy(backs[0].at[pl.ds(n * half, half)], buf.at[pl.ds(n * half, half)], sems.at[1 + n])
            for n in range(2)
        ]
        start_all(loads)
        for n, load in enumerate(loads):
            load.wait()
            for slot in range(n * half, (n + 1) * half):
                if full:
                    store(slot, buf.at[slot]).start()
                else:
                    pl.when(source_ref[slot] >= 0)(store(slot, buf.at[slot]).start)
    term.wait()
    grad[...] = (own[...] + far_ref[...].astype(jnp.float32)).astype(grad.dtype)
    write = pltpu.make_async_copy(grad, grad_hbm, sems.at[3])
    write.start()
    if full:
        pltpu.make_async_copy(out_hbm, out_hbm, out_sems.at[0]).wait()
    else:
        for slot in range(slots):
            pl.when(source_ref[slot] >= 0)(store(slot, buf.at[slot]).wait)
    write.wait()


def shards(tokens, cotangent, block_lang, counts, slot_of, ln_gain, w_down, w_up):
    block_count, block_rows, features = tokens.shape
    dp_size = lax.axis_size("dp")
    mp_size = lax.axis_size("mp")
    lang_local, bottleneck = w_down.shape[1:]
    shard = w_down.shape[0]
    width = lang_local * bottleneck
    capacity = (block_count + dp_size - 1) // dp_size
    slots = dp_size * capacity
    full = slots == block_count
    halves = block_rows // SLAB
    groups = capacity * halves
    lanes = 2 * groups * features + LANES
    rows = slots * block_rows
    tile = min(512, rows)
    resident = rows <= tile
    bf = jnp.bfloat16

    def shape(*extent, kind=bf):
        return jax.ShapeDtypeStruct(extent, kind)

    def vmem_shape(*extent, kind=bf):
        return pltpu.VMEM(extent, kind) if resident else shape(*extent, kind=kind)

    def in_vmem(*arrays):
        return [pltpu.with_memory_space_constraint(array, pltpu.VMEM) if resident else array for array in arrays]

    def in_hbm(*arrays):
        return [pltpu.with_memory_space_constraint(array, pltpu.HBM) for array in arrays]

    def swap(array, bit):
        return lax.ppermute(array, "mp", [(i, i ^ bit) for i in range(mp_size)])

    def exchange(array):
        return lax.all_to_all(array, "dp", split_axis=0, concat_axis=0, tiled=True)

    def swap_all(chunks):
        return [
            lax.ppermute(chunk, "dp", [(i, i ^ offset) for i in range(dp_size)]) if offset else chunk
            for offset, chunk in zip(OFFSETS, chunks)
        ]

    direct = OFFSETS if resident and dp_size == len(OFFSETS) else ()
    chunk_shape = [vmem_shape(SLAB, lanes)] * dp_size if direct else [pltpu.HBM((dp_size, SLAB, lanes), bf)]
    staging = [] if direct else [pltpu.VMEM((dp_size, SLAB, lanes), bf), pltpu.SemaphoreType.DMA(())]
    *packed, source = pl.pallas_call(
        functools.partial(pack_kernel, (dp_size, capacity, lang_local, full, direct)),
        out_shape=(*chunk_shape, shape(slots, kind=jnp.int32)),
        in_specs=[ANYWHERE] * 5,
        out_specs=(*([VMEM] * dp_size if direct else [ANYWHERE]), SMEM),
        scratch_shapes=[
            pltpu.VMEM(tokens.shape, bf),
            pltpu.VMEM(cotangent.shape, bf),
            pltpu.SMEM(block_lang.shape, jnp.int32),
            pltpu.SMEM(counts.shape, jnp.int32),
            pltpu.SMEM(slot_of.shape, jnp.int32),
            pltpu.SMEM((dp_size,), jnp.int32),
            pltpu.SemaphoreType.DMA((5,)),
            *staging,
        ],
        compiler_params=params(8 + slots // 4),
        name="pack",
    )(*in_hbm(block_lang, counts, slot_of, tokens, cotangent))

    gain_part = lax.dynamic_update_slice(
        jnp.zeros((SLAB, features), bf), ln_gain.T, (0, lax.axis_index("mp").astype(jnp.int32) * shard)
    )
    own = jnp.concatenate([w_down.reshape(shard, width), w_up.reshape(shard, width), gain_part], axis=0)
    core = swap(own, 1)
    pair = pl.pallas_call(
        pair_kernel,
        out_shape=vmem_shape(2 * own.shape[0], width),
        in_specs=[SMEM] + [ANYWHERE] * 2,
        out_specs=VMEM if resident else ANYWHERE,
        scratch_shapes=[pltpu.SemaphoreType.DMA((2,))],
        compiler_params=params(2 if resident else 8),
        name="pair",
    )(source, own, core)
    pair_far = swap(pair, 2)

    if direct:
        recv = swap_all(packed)
    else:
        recv = [exchange(packed[0])]
    inputs = in_vmem(*recv, pair, pair_far) if direct else in_hbm(*recv, pair, pair_far)

    part = vmem_shape(mp_size // 2, shard, width)
    up_keep, up_send, down_keep, down_send, *kept = pl.pallas_call(
        functools.partial(weight_grad_kernel, (capacity, mp_size, tile, 1.0 / (block_rows * mp_size), direct)),
        out_shape=(
            part,
            part,
            part,
            part,
            vmem_shape(rows, features),
            vmem_shape(rows, features),
            vmem_shape(rows, width),
            vmem_shape(rows, 2 * LANES, kind=jnp.float32),
            vmem_shape(rows, LANES, kind=jnp.float32),
            vmem_shape(features, width),
            vmem_shape(SLAB, features, kind=jnp.float32),
        ),
        in_specs=[VMEM if direct else ANYWHERE] * len(recv) + [ANYWHERE] * 2,
        out_specs=(VMEM,) * 11,
        scratch_shapes=[
            pltpu.VMEM((features, width), bf),
            pltpu.VMEM((mp_size, SLAB, features), bf),
            pltpu.VMEM((rows, features), bf),
            pltpu.VMEM((rows, width), bf),
            pltpu.SemaphoreType.DMA(()),
            pltpu.SemaphoreType.DMA((3, mp_size)),
            *staging[:1],
        ],
        compiler_params=params(14 + rows // 48),
        name="weight_grads",
    )(*inputs)

    tile = min(256, rows)
    chunk_rows = capacity * block_rows
    token_parts = pl.pallas_call(
        functools.partial(token_grad_kernel, tile, chunk_rows, direct),
        out_shape=[vmem_shape(chunk_rows, features)] * dp_size if direct else [pltpu.HBM((rows, features), bf)],
        in_specs=[VMEM] * 7,
        out_specs=[VMEM] * dp_size if direct else [ANYWHERE],
        scratch_shapes=[] if direct else [pltpu.VMEM((rows, features), bf), pltpu.SemaphoreType.DMA(())],
        compiler_params=params(4 + rows // 64),
        name="token_grads",
    )(*in_vmem(*kept))

    up_near, down_near = swap(up_send, 1), swap(down_send, 1)
    after = in_vmem(token_parts[0]) if direct else in_hbm(token_parts[0])
    *through, up_sum = pl.pallas_call(
        up_add_kernel,
        out_shape=(*[pltpu.HBM(array.shape, array.dtype) for array in after if not direct], vmem_shape(shard, width)),
        in_specs=[VMEM] * 2 + [ANYWHERE],
        out_specs=(*[ANYWHERE for _ in after if not direct], VMEM),
        input_output_aliases={} if direct else {2: 0},
        compiler_params=params(4),
        name="up_add",
    )(*in_vmem(up_keep, up_near), *after)
    down_sum, down_own = pl.pallas_call(
        down_add_kernel,
        out_shape=(
            vmem_shape(shard, lang_local, bottleneck),
            shape(shard, lang_local, bottleneck, kind=jnp.float32),
        ),
        in_specs=[VMEM] * 2,
        out_specs=(VMEM,) * 2,
        compiler_params=params(12),
        name="down_add",
    )(*in_vmem(down_keep, down_near))
    up_far, down_far = swap(up_sum, 2), swap(down_sum, 2)
    if direct:
        backs = in_vmem(*swap_all(token_parts))
    else:
        backs = in_hbm(exchange(through[0].reshape(slots, block_rows, features)))
    grad_shape = shape(shard, lang_local, bottleneck)
    grad_up = pl.pallas_call(
        finish_grad,
        out_shape=grad_shape,
        in_specs=[VMEM] * 3,
        out_specs=VMEM,
        compiler_params=params(8),
        name="up_finish",
    )(*in_hbm(up_keep, up_near, up_far))
    token_grad, grad_down = pl.pallas_call(
        functools.partial(tail_kernel, (capacity, full, direct)),
        out_shape=(shape(*tokens.shape), grad_shape),
        in_specs=[SMEM, ANYWHERE, VMEM] + [VMEM if direct else ANYWHERE] * len(backs),
        out_specs=(ANYWHERE, ANYWHERE),
        scratch_shapes=[
            pltpu.VMEM(grad_shape.shape, jnp.float32),
            pltpu.VMEM(grad_shape.shape, bf),
            pltpu.SemaphoreType.DMA((4,)),
            pltpu.SemaphoreType.DMA((slots,)),
            *([] if direct else [pltpu.VMEM((slots, block_rows, features), bf)]),
        ],
        compiler_params=params(8 + slots // 8),
        name="tail",
    )(source, *in_hbm(down_own), *in_vmem(down_far), *backs)
    return (token_grad, grad_down, grad_up)


def solution(mesh):
    placed = (
        P("dp", "mp", None),
        P("dp", "mp", None),
        P("dp"),
        P("dp"),
        P(),
        P("mp", "dp"),
        P("mp", "dp", None),
        P("mp", "dp", None),
    )
    return jax.shard_map(
        shards,
        mesh=mesh,
        in_specs=placed,
        out_specs=(P("dp", "mp", None), P("mp", "dp", None), P("mp", "dp", None)),
        check_vma=False,
    )
```

```python
import functools
import math

import jax
import jax.numpy as jnp
from jax import lax
from jax.experimental import pallas as pl
from jax.experimental.pallas import tpu as pltpu
from jax.sharding import PartitionSpec as P

SLAB = 16
LANES = 128
MIB = 1024 * 1024
OFFSETS = (0, 4, 1, 5, 2, 6, 3, 7)
ANYWHERE = pl.BlockSpec(memory_space=pl.ANY)
VMEM = pl.BlockSpec(memory_space=pltpu.VMEM)
SMEM = pl.BlockSpec(memory_space=pltpu.SMEM)


def params(mib):
    return pltpu.CompilerParams(vmem_limit_bytes=min(mib, 60) * MIB)


def start_all(copies):
    for copy in copies:
        copy.start()


def wait_all(copies):
    for copy in copies:
        copy.wait()


def pair_kernel(after_ref, own_hbm, core_hbm, out_ref, sems):
    size = own_hbm.shape[0]
    copies = [
        pltpu.make_async_copy(src, out_ref.at[pl.ds(n * size, size)], sems.at[n])
        for n, src in enumerate((own_hbm, core_hbm))
    ]
    start_all(copies)
    wait_all(copies)


def pack_kernel(dims, lang_hbm, count_hbm, slot_hbm, x_hbm, dy_hbm, *refs):
    dp_size, capacity, lang_local, full, direct = dims
    chunks, (source_ref, *scratch) = (refs[:dp_size], refs[dp_size:]) if direct else (None, refs[1:])
    block_count, block_rows, features = x_hbm.shape
    slots = dp_size * capacity
    halves = block_rows // SLAB
    x_buf, dy_buf, lang_ref, count_ref, slot_ref, taken_ref, sems, *scratch = scratch
    if not direct:
        out_hbm, (packed, out_sem) = refs[0], scratch
    loads = [
        pltpu.make_async_copy(src, dst, sems.at[n])
        for n, (src, dst) in enumerate(
            (
                (lang_hbm, lang_ref),
                (count_hbm, count_ref),
                (slot_hbm, slot_ref),
                (x_hbm, x_buf),
                (dy_hbm, dy_buf),
            )
        )
    ]
    start_all(loads)

    def clear_owner(owner, carry):
        taken_ref[owner] = 0
        return carry

    def clear_slot(slot, carry):
        source_ref[slot] = -1
        return carry

    lax.fori_loop(0, dp_size, clear_owner, 0, unroll=dp_size <= 8)
    if not full:
        lax.fori_loop(0, slots, clear_slot, 0)
    wait_all(loads[:3])

    def place(block, carry):
        owner = slot_ref[lang_ref[block]] // lang_local
        rank = taken_ref[owner]
        taken_ref[owner] = rank + 1
        source_ref[owner * capacity + rank] = block
        return carry

    lax.fori_loop(0, block_count, place, 0, unroll=True)
    wait_all(loads[3:])
    row_start = lax.axis_index("mp") * block_rows
    dy_groups = capacity * halves
    lane = lax.broadcasted_iota(jnp.int32, (SLAB, LANES), 1)

    def lanes_of(group):
        return pl.ds(group * features, features)

    def fill(out, block, place_in):
        live = count_ref[block] - row_start
        for half in range(halves):
            here = pl.ds(half * SLAB, SLAB)
            group = place_in * halves + half
            out[:, lanes_of(group)] = x_buf[block, here, :]
            rows = lax.broadcasted_iota(jnp.int32, (SLAB, features), 0) + half * SLAB
            piece = dy_buf[block, here, :].astype(jnp.float32)
            out[:, lanes_of(dy_groups + group)] = jnp.where(rows < live, piece, 0.0).astype(jnp.bfloat16)

    def blank(out, place_in):
        for half in range(halves):
            for base in (0, dy_groups):
                group = base + place_in * halves + half
                out[:, lanes_of(group)] = jnp.zeros((SLAB, features), jnp.bfloat16)

    def one_peer(out, peer):
        tags = jnp.zeros((SLAB, LANES), jnp.int32)
        for place_in in range(capacity):
            block = source_ref[peer * capacity + place_in]
            if full:
                fill(out, block, place_in)
            else:
                pl.when(block >= 0)(functools.partial(fill, out, block, place_in))
                pl.when(block < 0)(functools.partial(blank, out, place_in))
                block = jnp.maximum(block, 0)
            local = slot_ref[lang_ref[block]] % lang_local
            tags = jnp.where(lane // (LANES // capacity) == place_in, local, tags)
        out[:, pl.ds(2 * dy_groups * features, LANES)] = tags.astype(jnp.float32).astype(jnp.bfloat16)

    if direct:
        for offset, out in zip(direct, chunks):
            one_peer(out, lax.axis_index("dp") ^ offset)
    else:

        def send_peer(peer, carry):
            one_peer(packed.at[peer], peer)
            pltpu.make_async_copy(packed.at[peer], out_hbm.at[peer], out_sem).start()
            return carry

        lax.fori_loop(0, dp_size, send_peer, 0)
        pltpu.make_async_copy(packed, out_hbm, out_sem).wait()


def spread(values, second):
    return jnp.concatenate([jnp.where(second, 0.0, values), jnp.where(second, values, 0.0)], axis=1).astype(jnp.bfloat16)


def pick(values, second):
    half = values.shape[1] // 2
    return jnp.where(second, values[:, half:], values[:, :half])


def wide(column):
    return jnp.broadcast_to(column, (column.shape[0], LANES))


def gains_of(gain_ref, second):
    return jnp.where(second, gain_ref[1:2, :], gain_ref[0:1, :])


def normalize(values, second, gain_ref):
    values = values.astype(jnp.float32)
    row_mean = jnp.mean(values, axis=-1, keepdims=True)
    centered = values - row_mean
    inv_std = lax.rsqrt(jnp.mean(centered * centered, axis=-1, keepdims=True) + 1e-05)
    normed = (centered * inv_std * gains_of(gain_ref, second)).astype(jnp.bfloat16)
    return row_mean, inv_std, normed


def middle(masked, inner, second, up_ref):
    bell = 0.5 * (1.0 + lax.erf(inner * (1.0 / math.sqrt(2.0))))
    slope = bell + inner * jnp.exp(-0.5 * inner * inner) * (1.0 / math.sqrt(2.0 * math.pi))
    grad_act = pick(jnp.dot(masked, up_ref[...], preferred_element_type=jnp.float32), second)
    return spread(inner * bell, second), spread(grad_act * slope, second)


def backward(values, masked, row_mean, inv_std, second, grad_inner, gain_ref, down_ref):
    grad_normed = lax.dot_general(
        grad_inner, down_ref[...], (((1,), (1,)), ((), ())), preferred_element_type=jnp.float32
    )
    unit = (values.astype(jnp.float32) - row_mean) * inv_std
    scaled = grad_normed * gains_of(gain_ref, second)
    token_grad = masked.astype(jnp.float32) + inv_std * (
        scaled - jnp.mean(scaled, axis=-1, keepdims=True) - unit * jnp.mean(scaled * unit, axis=-1, keepdims=True)
    )
    return token_grad.astype(jnp.bfloat16)


def weight_grad_kernel(dims, *refs):
    capacity, mp_size, tile, scale, direct = dims
    source_count = len(direct) or 1
    sources, (pair_hbm, far_hbm), refs = refs[:source_count], refs[source_count:][:2], refs[source_count + 2 :]
    send_ref, x_buf, dy_buf, inner_buf, stats_buf, id_buf, down_ref, gain_ref, normed_buf, act_buf = refs[:10]
    up_ref, gain_buf, sems, weight_sems, *scratch = refs[10:]
    rows, features = x_buf.shape
    shard = features // mp_size
    first, then, later = [], [], []
    if direct:
        raw = sources
        chunks = len(direct)
    else:
        (raw,) = scratch
        chunks = raw.shape[0]
    groups = rows // (chunks * SLAB)
    split = groups * features
    if not direct:
        first.append(pltpu.make_async_copy(sources[0], raw, sems))
    size = pair_hbm.shape[0] // 2
    for offset in range(mp_size):
        weight, start = (pair_hbm, far_hbm)[offset // 2], offset % 2 * size
        here = pl.ds(pl.multiple_of((lax.axis_index("mp") ^ offset) * shard, shard), shard)
        for n, (group, src, dst) in enumerate(
            (
                (first, weight.at[pl.ds(start + 2 * shard, SLAB)], gain_buf.at[offset]),
                (then, weight.at[pl.ds(start, shard)], down_ref.at[here]),
                (later, weight.at[pl.ds(start + shard, shard)], up_ref.at[here]),
            )
        ):
            group.append(pltpu.make_async_copy(src, dst, weight_sems.at[n, offset]))
    start_all(first)
    start_all(then)
    start_all(later)
    wait_all(first)
    gain = gain_buf[0].astype(jnp.float32)
    for offset in range(1, mp_size):
        gain = gain + gain_buf[offset].astype(jnp.float32)
    gain_ref[...] = gain
    tile_chunks = tile // (groups * SLAB)
    per_block = groups // capacity

    def chunk_of(step, chunk):
        return raw[chunk] if direct else raw.at[step * tile_chunks + chunk]

    def rows_of(step, base):
        return jnp.concatenate(
            [
                chunk_of(step, chunk)[:, pl.ds((base + group) * features, features)]
                for chunk in range(tile_chunks)
                for group in range(groups)
            ],
            axis=0,
        )

    def ids_of(step):
        pieces = []
        for chunk in range(tile_chunks):
            tags = chunk_of(step, chunk)[:, pl.ds(2 * split, LANES)].astype(jnp.float32)
            for group in range(groups):
                column = (group // per_block) * (LANES // capacity)
                pieces.append(wide(tags[:, column : column + 1]))
        return jnp.concatenate(pieces, axis=0)

    whole = rows == tile
    if not whole:
        wait_all(then + later)

    def one_tile(step, carry):
        here = pl.ds(pl.multiple_of(step * tile, tile), tile)
        ids = ids_of(step)
        id_buf[here, :] = ids
        second = ids[:, :1] > 0.5
        values = rows_of(step, 0)
        x_buf[here, :] = values
        row_mean, inv_std, normed = normalize(values, second, gain_ref)
        normed_buf[here, :] = normed
        stats_buf[here, :] = jnp.concatenate([wide(row_mean), wide(inv_std)], axis=1)
        if whole:
            wait_all(then)
        inner = pick(jnp.dot(normed_buf[here, :], down_ref[...], preferred_element_type=jnp.float32), second)
        if whole:
            wait_all(later)
        dy_buf[here, :] = rows_of(step, groups)
        act, grad_inner = middle(dy_buf[here, :], inner, second, up_ref)
        act_buf[here, :] = act
        inner_buf[here, :] = grad_inner
        return carry

    if whole:
        one_tile(0, 0)
    else:
        lax.fori_loop(0, rows // tile, one_tile, 0)
    products(dy_buf, act_buf, normed_buf, inner_buf, send_ref, 1, scale)


def products(dy_ref, act_ref, normed_ref, inner_ref, out_ref, first, scale):
    half, _, shard, _ = out_ref.shape
    for n in range(half):
        here = pl.ds(pl.multiple_of((lax.axis_index("mp") ^ (2 * n + first)) * shard, shard), shard)
        for kind, (left, right) in enumerate(((dy_ref, act_ref), (normed_ref, inner_ref))):
            part = lax.dot_general(
                left[:, here], right[...], (((0,), (0,)), ((), ())), preferred_element_type=jnp.float32
            )
            out_ref[n, kind] = (part * scale).astype(jnp.bfloat16)


def token_grad_kernel(
    dims, x_ref, dy_ref, inner_ref, stats_ref, id_ref, down_ref, gain_ref, normed_ref, act_ref, keep_ref, *refs
):
    tile, chunk_rows, direct, scale = dims
    rows = x_ref.shape[0]

    def part(here):
        stats = stats_ref[here, :]
        return backward(
            x_ref[here, :],
            dy_ref[here, :],
            stats[:, :1],
            stats[:, LANES : LANES + 1],
            id_ref[here, :][:, :1] > 0.5,
            inner_ref[here, :],
            gain_ref,
            down_ref,
        )

    if direct:
        for step in range(rows // tile):
            token_grad = part(pl.ds(step * tile, tile))
            for n in range(tile // chunk_rows):
                refs[step * (tile // chunk_rows) + n][...] = token_grad[n * chunk_rows : (n + 1) * chunk_rows]
        products(dy_ref, act_ref, normed_ref, inner_ref, keep_ref, 0, scale)
        return
    out_hbm, grad_buf, sem = refs

    def one_tile(step, carry):
        here = pl.ds(pl.multiple_of(step * tile, tile), tile)
        grad_buf[here, :] = part(here)
        pltpu.make_async_copy(grad_buf.at[here], out_hbm.at[here], sem).start()
        return carry

    lax.fori_loop(0, rows // tile, one_tile, 0)
    products(dy_ref, act_ref, normed_ref, inner_ref, keep_ref, 0, scale)
    pltpu.make_async_copy(grad_buf, out_hbm, sem).wait()


def add_kernel(place, keep_ref, near_ref, out_ref):
    for kind in range(keep_ref.shape[1]):
        total = keep_ref[place, kind].astype(jnp.float32) + near_ref[place, kind].astype(jnp.float32)
        out_ref[kind] = total.reshape(out_ref.shape[1:]).astype(out_ref.dtype)


def tail_kernel(dims, source_ref, own_ref, far_ref, *refs):
    capacity, full, direct = dims
    back_count = len(direct) or 1
    backs, (out_hbm, *grad_hbms, grad, sems, out_sems), buf = (
        refs[:back_count],
        refs[back_count : back_count + 6],
        refs[back_count + 6 :],
    )
    slots = out_sems.shape[0]
    block_rows = out_hbm.shape[1]
    half = slots // 2

    def store(slot, piece):
        if full:
            return pltpu.make_async_copy(piece, out_hbm.at[source_ref[slot]], out_sems.at[0])
        return pltpu.make_async_copy(piece, out_hbm.at[jnp.maximum(source_ref[slot], 0)], out_sems.at[slot])

    if direct:
        for offset, back in zip(direct, backs):
            for place_in in range(capacity):
                slot = (lax.axis_index("dp") ^ offset) * capacity + place_in
                store(slot, back.at[pl.ds(place_in * block_rows, block_rows)]).start()
    else:
        (buf,) = buf
        loads = [
            pltpu.make_async_copy(backs[0].at[pl.ds(n * half, half)], buf.at[pl.ds(n * half, half)], sems.at[n])
            for n in range(2)
        ]
        start_all(loads)
        for n, load in enumerate(loads):
            load.wait()
            for slot in range(n * half, (n + 1) * half):
                if full:
                    store(slot, buf.at[slot]).start()
                else:
                    pl.when(source_ref[slot] >= 0)(store(slot, buf.at[slot]).start)
    writes = []
    for kind, grad_hbm in enumerate(grad_hbms):
        grad[kind] = (own_ref[kind] + far_ref[kind].astype(jnp.float32)).astype(grad.dtype)
        writes.append(pltpu.make_async_copy(grad.at[kind], grad_hbm, sems.at[2 + kind]))
        writes[-1].start()
    if full:
        pltpu.make_async_copy(out_hbm, out_hbm, out_sems.at[0]).wait()
    else:
        for slot in range(slots):
            pl.when(source_ref[slot] >= 0)(store(slot, buf.at[slot]).wait)
    wait_all(writes)


def shards(tokens, cotangent, block_lang, counts, slot_of, ln_gain, w_down, w_up):
    block_count, block_rows, features = tokens.shape
    dp_size = lax.axis_size("dp")
    mp_size = lax.axis_size("mp")
    lang_local, bottleneck = w_down.shape[1:]
    shard = w_down.shape[0]
    width = lang_local * bottleneck
    capacity = (block_count + dp_size - 1) // dp_size
    slots = dp_size * capacity
    full = slots == block_count
    halves = block_rows // SLAB
    groups = capacity * halves
    lanes = 2 * groups * features + LANES
    rows = slots * block_rows
    tile = min(512, rows)
    resident = rows <= tile
    bf = jnp.bfloat16

    def shape(*extent, kind=bf):
        return jax.ShapeDtypeStruct(extent, kind)

    def vmem_shape(*extent, kind=bf):
        return pltpu.VMEM(extent, kind) if resident else shape(*extent, kind=kind)

    def in_vmem(*arrays):
        return [pltpu.with_memory_space_constraint(array, pltpu.VMEM) if resident else array for array in arrays]

    def in_hbm(*arrays):
        return [pltpu.with_memory_space_constraint(array, pltpu.HBM) for array in arrays]

    def swap(array, bit):
        return lax.ppermute(array, "mp", [(i, i ^ bit) for i in range(mp_size)])

    def exchange(array):
        return lax.all_to_all(array, "dp", split_axis=0, concat_axis=0, tiled=True)

    def swap_all(chunks):
        return [
            lax.ppermute(chunk, "dp", [(i, i ^ offset) for i in range(dp_size)]) if offset else chunk
            for offset, chunk in zip(OFFSETS, chunks)
        ]

    direct = OFFSETS if resident and dp_size == len(OFFSETS) else ()
    chunk_shape = [vmem_shape(SLAB, lanes)] * dp_size if direct else [pltpu.HBM((dp_size, SLAB, lanes), bf)]
    staging = [] if direct else [pltpu.VMEM((dp_size, SLAB, lanes), bf), pltpu.SemaphoreType.DMA(())]
    *packed, source = pl.pallas_call(
        functools.partial(pack_kernel, (dp_size, capacity, lang_local, full, direct)),
        out_shape=(*chunk_shape, shape(slots, kind=jnp.int32)),
        in_specs=[ANYWHERE] * 5,
        out_specs=(*([VMEM] * dp_size if direct else [ANYWHERE]), SMEM),
        scratch_shapes=[
            pltpu.VMEM(tokens.shape, bf),
            pltpu.VMEM(cotangent.shape, bf),
            pltpu.SMEM(block_lang.shape, jnp.int32),
            pltpu.SMEM(counts.shape, jnp.int32),
            pltpu.SMEM(slot_of.shape, jnp.int32),
            pltpu.SMEM((dp_size,), jnp.int32),
            pltpu.SemaphoreType.DMA((5,)),
            *staging,
        ],
        compiler_params=params(8 + slots // 4),
        name="pack",
    )(*in_hbm(block_lang, counts, slot_of, tokens, cotangent))

    gain_part = lax.dynamic_update_slice(
        jnp.zeros((SLAB, features), bf), ln_gain.T, (0, lax.axis_index("mp").astype(jnp.int32) * shard)
    )
    own = jnp.concatenate([w_down.reshape(shard, width), w_up.reshape(shard, width), gain_part], axis=0)
    core = swap(own, 1)
    pair = pl.pallas_call(
        pair_kernel,
        out_shape=vmem_shape(2 * own.shape[0], width),
        in_specs=[SMEM] + [ANYWHERE] * 2,
        out_specs=VMEM if resident else ANYWHERE,
        scratch_shapes=[pltpu.SemaphoreType.DMA((2,))],
        compiler_params=params(2 if resident else 8),
        name="pair",
    )(source, own, core)
    pair_far = swap(pair, 2)

    if direct:
        recv = swap_all(packed)
    else:
        recv = [exchange(packed[0])]
    inputs = in_vmem(*recv, pair, pair_far) if direct else in_hbm(*recv, pair, pair_far)

    part = vmem_shape(mp_size // 2, 2, shard, width)
    scale = 1.0 / (block_rows * mp_size)
    send, *kept = pl.pallas_call(
        functools.partial(weight_grad_kernel, (capacity, mp_size, tile, scale, direct)),
        out_shape=(
            part,
            vmem_shape(rows, features),
            vmem_shape(rows, features),
            vmem_shape(rows, width),
            vmem_shape(rows, 2 * LANES, kind=jnp.float32),
            vmem_shape(rows, LANES, kind=jnp.float32),
            vmem_shape(features, width),
            vmem_shape(SLAB, features, kind=jnp.float32),
            vmem_shape(rows, features),
            vmem_shape(rows, width),
        ),
        in_specs=[VMEM if direct else ANYWHERE] * len(recv) + [ANYWHERE] * 2,
        out_specs=(VMEM,) * 10,
        scratch_shapes=[
            pltpu.VMEM((features, width), bf),
            pltpu.VMEM((mp_size, SLAB, features), bf),
            pltpu.SemaphoreType.DMA(()),
            pltpu.SemaphoreType.DMA((3, mp_size)),
            *staging[:1],
        ],
        compiler_params=params(14 + rows // 48),
        name="weight_grads",
    )(*inputs)
    near = swap(send, 1)

    tile = min(256, rows)
    chunk_rows = capacity * block_rows
    keep, *token_parts = pl.pallas_call(
        functools.partial(token_grad_kernel, (tile, chunk_rows, direct, scale)),
        out_shape=[
            part,
            *([vmem_shape(chunk_rows, features)] * dp_size if direct else [pltpu.HBM((rows, features), bf)]),
        ],
        in_specs=[VMEM] * 9,
        out_specs=[VMEM] * (1 + dp_size) if direct else [VMEM, ANYWHERE],
        scratch_shapes=[] if direct else [pltpu.VMEM((rows, features), bf), pltpu.SemaphoreType.DMA(())],
        compiler_params=params(12 + rows // 64),
        name="token_grads",
    )(*in_vmem(*kept))

    def add(place, kind, name):
        return pl.pallas_call(
            functools.partial(add_kernel, place),
            out_shape=vmem_shape(2, shard, lang_local, bottleneck, kind=kind),
            in_specs=[VMEM] * 2,
            out_specs=VMEM,
            compiler_params=params(14),
            name=name,
        )(*in_vmem(keep, near))

    far = swap(add(1, bf, "far_add"), 2)
    own_sum = add(0, jnp.float32, "own_add")
    if direct:
        backs = in_vmem(*swap_all(token_parts))
    else:
        backs = in_hbm(exchange(token_parts[0].reshape(slots, block_rows, features)))
    grad_shape = shape(shard, lang_local, bottleneck)
    token_grad, grad_up, grad_down = pl.pallas_call(
        functools.partial(tail_kernel, (capacity, full, direct)),
        out_shape=(shape(*tokens.shape), grad_shape, grad_shape),
        in_specs=[SMEM] + [VMEM] * 2 + [VMEM if direct else ANYWHERE] * len(backs),
        out_specs=(ANYWHERE,) * 3,
        scratch_shapes=[
            pltpu.VMEM((2, shard, lang_local, bottleneck), bf),
            pltpu.SemaphoreType.DMA((4,)),
            pltpu.SemaphoreType.DMA((slots,)),
            *([] if direct else [pltpu.VMEM((slots, block_rows, features), bf)]),
        ],
        compiler_params=params(8 + slots // 4),
        name="tail",
    )(source, *in_vmem(own_sum, far), *backs)
    return (token_grad, grad_down, grad_up)


def solution(mesh):
    placed = (
        P("dp", "mp", None),
        P("dp", "mp", None),
        P("dp"),
        P("dp"),
        P(),
        P("mp", "dp"),
        P("mp", "dp", None),
        P("mp", "dp", None),
    )
    return jax.shard_map(
        shards,
        mesh=mesh,
        in_specs=placed,
        out_specs=(P("dp", "mp", None), P("mp", "dp", None), P("mp", "dp", None)),
        check_vma=False,
    )
```

```python
import functools
import math

import jax
import jax.numpy as jnp
from jax import lax
from jax.experimental import pallas as pl
from jax.experimental.pallas import tpu as pltpu
from jax.sharding import PartitionSpec as P

SLAB = 16
LANES = 128
MIB = 1024 * 1024
OFFSETS = (0, 4, 1, 5, 2, 6, 3, 7)
ANYWHERE = pl.BlockSpec(memory_space=pl.ANY)
VMEM = pl.BlockSpec(memory_space=pltpu.VMEM)
SMEM = pl.BlockSpec(memory_space=pltpu.SMEM)


def params(mib):
    return pltpu.CompilerParams(vmem_limit_bytes=min(mib, 60) * MIB)


def start_all(copies):
    for copy in copies:
        copy.start()


def wait_all(copies):
    for copy in copies:
        copy.wait()


def load_kernel(down_hbm, up_hbm, down_ref, up_ref, sems):
    copies = [
        pltpu.make_async_copy(src, dst, sems.at[n])
        for n, (src, dst) in enumerate(((down_hbm, down_ref), (up_hbm, up_ref)))
    ]
    start_all(copies)
    wait_all(copies)


def pair_kernel(after_ref, own_hbm, core_hbm, out_ref, sems):
    size = own_hbm.shape[0]
    copies = [
        pltpu.make_async_copy(src, out_ref.at[pl.ds(n * size, size)], sems.at[n])
        for n, src in enumerate((own_hbm, core_hbm))
    ]
    start_all(copies)
    wait_all(copies)


def pack_kernel(dims, lang_hbm, count_hbm, slot_hbm, x_hbm, dy_hbm, *refs):
    dp_size, capacity, lang_local, full, direct = dims
    chunks, (source_ref, *scratch) = (refs[:dp_size], refs[dp_size:]) if direct else (None, refs[1:])
    block_count, block_rows, features = x_hbm.shape
    slots = dp_size * capacity
    halves = block_rows // SLAB
    x_buf, dy_buf, lang_ref, count_ref, slot_ref, taken_ref, sems, *scratch = scratch
    if not direct:
        out_hbm, (packed, out_sem) = refs[0], scratch
    loads = [
        pltpu.make_async_copy(src, dst, sems.at[n])
        for n, (src, dst) in enumerate(
            (
                (lang_hbm, lang_ref),
                (count_hbm, count_ref),
                (slot_hbm, slot_ref),
                (x_hbm, x_buf),
                (dy_hbm, dy_buf),
            )
        )
    ]
    start_all(loads)

    def clear_owner(owner, carry):
        taken_ref[owner] = 0
        return carry

    def clear_slot(slot, carry):
        source_ref[slot] = -1
        return carry

    lax.fori_loop(0, dp_size, clear_owner, 0, unroll=dp_size <= 8)
    if not full:
        lax.fori_loop(0, slots, clear_slot, 0)
    wait_all(loads[:3])

    def place(block, carry):
        owner = slot_ref[lang_ref[block]] // lang_local
        rank = taken_ref[owner]
        taken_ref[owner] = rank + 1
        source_ref[owner * capacity + rank] = block
        return carry

    lax.fori_loop(0, block_count, place, 0, unroll=True)
    wait_all(loads[3:])
    row_start = lax.axis_index("mp") * block_rows
    dy_groups = capacity * halves
    lane = lax.broadcasted_iota(jnp.int32, (SLAB, LANES), 1)

    def lanes_of(group):
        return pl.ds(group * features, features)

    def fill(out, block, place_in):
        live = count_ref[block] - row_start
        for half in range(halves):
            here = pl.ds(half * SLAB, SLAB)
            group = place_in * halves + half
            out[:, lanes_of(group)] = x_buf[block, here, :]
            rows = lax.broadcasted_iota(jnp.int32, (SLAB, features), 0) + half * SLAB
            piece = dy_buf[block, here, :].astype(jnp.float32)
            out[:, lanes_of(dy_groups + group)] = jnp.where(rows < live, piece, 0.0).astype(jnp.bfloat16)

    def blank(out, place_in):
        for half in range(halves):
            for base in (0, dy_groups):
                group = base + place_in * halves + half
                out[:, lanes_of(group)] = jnp.zeros((SLAB, features), jnp.bfloat16)

    def one_peer(out, peer):
        tags = jnp.zeros((SLAB, LANES), jnp.int32)
        for place_in in range(capacity):
            block = source_ref[peer * capacity + place_in]
            if full:
                fill(out, block, place_in)
            else:
                pl.when(block >= 0)(functools.partial(fill, out, block, place_in))
                pl.when(block < 0)(functools.partial(blank, out, place_in))
                block = jnp.maximum(block, 0)
            local = slot_ref[lang_ref[block]] % lang_local
            tags = jnp.where(lane // (LANES // capacity) == place_in, local, tags)
        out[:, pl.ds(2 * dy_groups * features, LANES)] = tags.astype(jnp.float32).astype(jnp.bfloat16)

    if direct:
        for offset, out in zip(direct, chunks):
            one_peer(out, lax.axis_index("dp") ^ offset)
    else:

        def send_peer(peer, carry):
            one_peer(packed.at[peer], peer)
            pltpu.make_async_copy(packed.at[peer], out_hbm.at[peer], out_sem).start()
            return carry

        lax.fori_loop(0, dp_size, send_peer, 0)
        pltpu.make_async_copy(packed, out_hbm, out_sem).wait()


def spread(values, second):
    return jnp.concatenate([jnp.where(second, 0.0, values), jnp.where(second, values, 0.0)], axis=1).astype(jnp.bfloat16)


def pick(values, second):
    half = values.shape[1] // 2
    return jnp.where(second, values[:, half:], values[:, :half])


def wide(column):
    return jnp.broadcast_to(column, (column.shape[0], LANES))


def gains_of(gain_ref, second):
    return jnp.where(second, gain_ref[1:2, :], gain_ref[0:1, :])


def normalize(values, second, gain_ref):
    values = values.astype(jnp.float32)
    row_mean = jnp.mean(values, axis=-1, keepdims=True)
    centered = values - row_mean
    inv_std = lax.rsqrt(jnp.mean(centered * centered, axis=-1, keepdims=True) + 1e-05)
    normed = (centered * inv_std * gains_of(gain_ref, second)).astype(jnp.bfloat16)
    return row_mean, inv_std, normed


def middle(masked, inner, second, up_ref):
    bell = 0.5 * (1.0 + lax.erf(inner * (1.0 / math.sqrt(2.0))))
    slope = bell + inner * jnp.exp(-0.5 * inner * inner) * (1.0 / math.sqrt(2.0 * math.pi))
    grad_act = pick(jnp.dot(masked, up_ref[...], preferred_element_type=jnp.float32), second)
    return spread(inner * bell, second), spread(grad_act * slope, second)


def backward(values, masked, row_mean, inv_std, second, grad_inner, gain_ref, down_ref):
    grad_normed = lax.dot_general(
        grad_inner, down_ref[...], (((1,), (1,)), ((), ())), preferred_element_type=jnp.float32
    )
    unit = (values.astype(jnp.float32) - row_mean) * inv_std
    scaled = grad_normed * gains_of(gain_ref, second)
    token_grad = masked.astype(jnp.float32) + inv_std * (
        scaled - jnp.mean(scaled, axis=-1, keepdims=True) - unit * jnp.mean(scaled * unit, axis=-1, keepdims=True)
    )
    return token_grad.astype(jnp.bfloat16)


def weight_grad_kernel(dims, *refs):
    capacity, mp_size, tile, scale, direct = dims
    source_count = len(direct) or 1
    sources, (pair_hbm, far_hbm), refs = refs[:source_count], refs[source_count:][:2], refs[source_count + 2 :]
    send_ref, x_buf, dy_buf, inner_buf, stats_buf, id_buf, down_ref, gain_ref, normed_buf, act_buf = refs[:10]
    up_ref, gain_buf, sems, weight_sems, *scratch = refs[10:]
    rows, features = x_buf.shape
    shard = features // mp_size
    first, then, later = [], [], []
    if direct:
        raw = sources
        chunks = len(direct)
    else:
        (raw,) = scratch
        chunks = raw.shape[0]
    groups = rows // (chunks * SLAB)
    split = groups * features
    if not direct:
        first.append(pltpu.make_async_copy(sources[0], raw, sems))
    size = pair_hbm.shape[0] // 2
    for offset in range(mp_size):
        weight, start = (pair_hbm, far_hbm)[offset // 2], offset % 2 * size
        here = pl.ds(pl.multiple_of((lax.axis_index("mp") ^ offset) * shard, shard), shard)
        for n, (group, src, dst) in enumerate(
            (
                (first, weight.at[pl.ds(start + 2 * shard, SLAB)], gain_buf.at[offset]),
                (then, weight.at[pl.ds(start, shard)], down_ref.at[here]),
                (later, weight.at[pl.ds(start + shard, shard)], up_ref.at[here]),
            )
        ):
            group.append(pltpu.make_async_copy(src, dst, weight_sems.at[n, offset]))
    start_all(first)
    start_all(then)
    start_all(later)
    wait_all(first)
    for offset in range(mp_size):
        here = pl.ds(pl.multiple_of((lax.axis_index("mp") ^ offset) * shard, shard), shard)
        gain_ref[:, here] = gain_buf[offset, :, pl.ds(0, shard)].astype(jnp.float32)
    tile_chunks = tile // (groups * SLAB)
    per_block = groups // capacity

    def chunk_of(step, chunk):
        return raw[chunk] if direct else raw.at[step * tile_chunks + chunk]

    def rows_of(step, base):
        return jnp.concatenate(
            [
                chunk_of(step, chunk)[:, pl.ds((base + group) * features, features)]
                for chunk in range(tile_chunks)
                for group in range(groups)
            ],
            axis=0,
        )

    def ids_of(step):
        pieces = []
        for chunk in range(tile_chunks):
            tags = chunk_of(step, chunk)[:, pl.ds(2 * split, LANES)].astype(jnp.float32)
            for group in range(groups):
                column = (group // per_block) * (LANES // capacity)
                pieces.append(wide(tags[:, column : column + 1]))
        return jnp.concatenate(pieces, axis=0)

    whole = rows == tile
    if not whole:
        wait_all(then + later)

    def one_tile(step, carry):
        here = pl.ds(pl.multiple_of(step * tile, tile), tile)
        ids = ids_of(step)
        id_buf[here, :] = ids
        second = ids[:, :1] > 0.5
        values = rows_of(step, 0)
        x_buf[here, :] = values
        row_mean, inv_std, normed = normalize(values, second, gain_ref)
        normed_buf[here, :] = normed
        stats_buf[here, :] = jnp.concatenate([wide(row_mean), wide(inv_std)], axis=1)
        if whole:
            wait_all(then)
        inner = pick(jnp.dot(normed_buf[here, :], down_ref[...], preferred_element_type=jnp.float32), second)
        if whole:
            wait_all(later)
        dy_buf[here, :] = rows_of(step, groups)
        act, grad_inner = middle(dy_buf[here, :], inner, second, up_ref)
        act_buf[here, :] = act
        inner_buf[here, :] = grad_inner
        return carry

    if whole:
        one_tile(0, 0)
    else:
        lax.fori_loop(0, rows // tile, one_tile, 0)
    products(dy_buf, act_buf, normed_buf, inner_buf, send_ref, 1, scale)


def products(dy_ref, act_ref, normed_ref, inner_ref, out_ref, first, scale):
    half, _, shard, _ = out_ref.shape
    for n in range(half):
        here = pl.ds(pl.multiple_of((lax.axis_index("mp") ^ (2 * n + first)) * shard, shard), shard)
        for kind, (left, right) in enumerate(((dy_ref, act_ref), (normed_ref, inner_ref))):
            part = lax.dot_general(
                left[:, here], right[...], (((0,), (0,)), ((), ())), preferred_element_type=jnp.float32
            )
            out_ref[n, kind] = (part * scale).astype(jnp.bfloat16)


def token_grad_kernel(
    dims, x_ref, dy_ref, inner_ref, stats_ref, id_ref, down_ref, gain_ref, normed_ref, act_ref, keep_ref, *refs
):
    tile, chunk_rows, direct, scale = dims
    rows = x_ref.shape[0]

    def part(here):
        stats = stats_ref[here, :]
        return backward(
            x_ref[here, :],
            dy_ref[here, :],
            stats[:, :1],
            stats[:, LANES : LANES + 1],
            id_ref[here, :][:, :1] > 0.5,
            inner_ref[here, :],
            gain_ref,
            down_ref,
        )

    if direct:
        for step in range(rows // tile):
            token_grad = part(pl.ds(step * tile, tile))
            for n in range(tile // chunk_rows):
                refs[step * (tile // chunk_rows) + n][...] = token_grad[n * chunk_rows : (n + 1) * chunk_rows]
        products(dy_ref, act_ref, normed_ref, inner_ref, keep_ref, 0, scale)
        return
    out_hbm, grad_buf, sem = refs

    def one_tile(step, carry):
        here = pl.ds(pl.multiple_of(step * tile, tile), tile)
        grad_buf[here, :] = part(here)
        pltpu.make_async_copy(grad_buf.at[here], out_hbm.at[here], sem).start()
        return carry

    lax.fori_loop(0, rows // tile, one_tile, 0)
    products(dy_ref, act_ref, normed_ref, inner_ref, keep_ref, 0, scale)
    pltpu.make_async_copy(grad_buf, out_hbm, sem).wait()


def add_kernel(place, keep_ref, near_ref, out_ref):
    for kind in range(keep_ref.shape[1]):
        total = keep_ref[place, kind].astype(jnp.float32) + near_ref[place, kind].astype(jnp.float32)
        out_ref[kind] = total.reshape(out_ref.shape[1:]).astype(out_ref.dtype)


def tail_kernel(dims, source_ref, own_ref, far_ref, *refs):
    capacity, full, direct = dims
    back_count = len(direct) or 1
    backs, (out_hbm, *grad_hbms, grad, sems, out_sems), buf = (
        refs[:back_count],
        refs[back_count : back_count + 6],
        refs[back_count + 6 :],
    )
    slots = out_sems.shape[0]
    block_rows = out_hbm.shape[1]
    half = slots // 2

    def store(slot, piece):
        if full:
            return pltpu.make_async_copy(piece, out_hbm.at[source_ref[slot]], out_sems.at[0])
        return pltpu.make_async_copy(piece, out_hbm.at[jnp.maximum(source_ref[slot], 0)], out_sems.at[slot])

    if direct:
        for offset, back in zip(direct, backs):
            for place_in in range(capacity):
                slot = (lax.axis_index("dp") ^ offset) * capacity + place_in
                store(slot, back.at[pl.ds(place_in * block_rows, block_rows)]).start()
    else:
        (buf,) = buf
        loads = [
            pltpu.make_async_copy(backs[0].at[pl.ds(n * half, half)], buf.at[pl.ds(n * half, half)], sems.at[n])
            for n in range(2)
        ]
        start_all(loads)
        for n, load in enumerate(loads):
            load.wait()
            for slot in range(n * half, (n + 1) * half):
                if full:
                    store(slot, buf.at[slot]).start()
                else:
                    pl.when(source_ref[slot] >= 0)(store(slot, buf.at[slot]).start)
    writes = []
    for kind, grad_hbm in enumerate(grad_hbms):
        total = own_ref[kind] + far_ref[kind].astype(jnp.float32).reshape(grad.shape[1:])
        grad[kind] = total.astype(grad.dtype)
        writes.append(pltpu.make_async_copy(grad.at[kind], grad_hbm, sems.at[2 + kind]))
        writes[-1].start()
    if full:
        pltpu.make_async_copy(out_hbm, out_hbm, out_sems.at[0]).wait()
    else:
        for slot in range(slots):
            pl.when(source_ref[slot] >= 0)(store(slot, buf.at[slot]).wait)
    wait_all(writes)


def shards(tokens, cotangent, block_lang, counts, slot_of, ln_gain, w_down, w_up):
    block_count, block_rows, features = tokens.shape
    dp_size = lax.axis_size("dp")
    mp_size = lax.axis_size("mp")
    lang_local, bottleneck = w_down.shape[1:]
    shard = w_down.shape[0]
    width = lang_local * bottleneck
    capacity = (block_count + dp_size - 1) // dp_size
    slots = dp_size * capacity
    full = slots == block_count
    halves = block_rows // SLAB
    groups = capacity * halves
    lanes = 2 * groups * features + LANES
    rows = slots * block_rows
    tile = min(512, rows)
    resident = rows <= tile
    bf = jnp.bfloat16

    def shape(*extent, kind=bf):
        return jax.ShapeDtypeStruct(extent, kind)

    def vmem_shape(*extent, kind=bf):
        return pltpu.VMEM(extent, kind) if resident else shape(*extent, kind=kind)

    def in_vmem(*arrays):
        return [pltpu.with_memory_space_constraint(array, pltpu.VMEM) if resident else array for array in arrays]

    def in_hbm(*arrays):
        return [pltpu.with_memory_space_constraint(array, pltpu.HBM) for array in arrays]

    def swap(array, bit):
        return lax.ppermute(array, "mp", [(i, i ^ bit) for i in range(mp_size)])

    def exchange(array):
        return lax.all_to_all(array, "dp", split_axis=0, concat_axis=0, tiled=True)

    def swap_all(chunks):
        return [
            lax.ppermute(chunk, "dp", [(i, i ^ offset) for i in range(dp_size)]) if offset else chunk
            for offset, chunk in zip(OFFSETS, chunks)
        ]

    direct = OFFSETS if resident and dp_size == len(OFFSETS) else ()
    chunk_shape = [vmem_shape(SLAB, lanes)] * dp_size if direct else [pltpu.HBM((dp_size, SLAB, lanes), bf)]
    staging = [] if direct else [pltpu.VMEM((dp_size, SLAB, lanes), bf), pltpu.SemaphoreType.DMA(())]
    *packed, source = pl.pallas_call(
        functools.partial(pack_kernel, (dp_size, capacity, lang_local, full, direct)),
        out_shape=(*chunk_shape, shape(slots, kind=jnp.int32)),
        in_specs=[ANYWHERE] * 5,
        out_specs=(*([VMEM] * dp_size if direct else [ANYWHERE]), SMEM),
        scratch_shapes=[
            pltpu.VMEM(tokens.shape, bf),
            pltpu.VMEM(cotangent.shape, bf),
            pltpu.SMEM(block_lang.shape, jnp.int32),
            pltpu.SMEM(counts.shape, jnp.int32),
            pltpu.SMEM(slot_of.shape, jnp.int32),
            pltpu.SMEM((dp_size,), jnp.int32),
            pltpu.SemaphoreType.DMA((5,)),
            *staging,
        ],
        compiler_params=params(8 + slots // 4),
        name="pack",
    )(*in_hbm(block_lang, counts, slot_of, tokens, cotangent))

    down_raw, up_raw = pl.pallas_call(
        load_kernel,
        out_shape=(vmem_shape(*w_down.shape), vmem_shape(*w_up.shape)),
        in_specs=[ANYWHERE] * 2,
        out_specs=(VMEM if resident else ANYWHERE,) * 2,
        scratch_shapes=[pltpu.SemaphoreType.DMA((2,))],
        compiler_params=params(2),
        name="load",
    )(*in_hbm(w_down, w_up))
    gain_part = jnp.pad(ln_gain.T, ((0, SLAB - lang_local), (0, width - shard)))
    own = jnp.concatenate([down_raw.reshape(shard, width), up_raw.reshape(shard, width), gain_part], axis=0)
    core = swap(own, 1)
    pair = pl.pallas_call(
        pair_kernel,
        out_shape=vmem_shape(2 * own.shape[0], width),
        in_specs=[SMEM] + [ANYWHERE] * 2,
        out_specs=VMEM if resident else ANYWHERE,
        scratch_shapes=[pltpu.SemaphoreType.DMA((2,))],
        compiler_params=params(2 if resident else 8),
        name="pair",
    )(source, own, core)
    pair_far = swap(pair, 2)

    if direct:
        recv = swap_all(packed)
    else:
        recv = [exchange(packed[0])]
    inputs = in_vmem(*recv, pair, pair_far) if direct else in_hbm(*recv, pair, pair_far)

    part = vmem_shape(mp_size // 2, 2, shard, width)
    scale = 1.0 / (block_rows * mp_size)
    send, *kept = pl.pallas_call(
        functools.partial(weight_grad_kernel, (capacity, mp_size, tile, scale, direct)),
        out_shape=(
            part,
            vmem_shape(rows, features),
            vmem_shape(rows, features),
            vmem_shape(rows, width),
            vmem_shape(rows, 2 * LANES, kind=jnp.float32),
            vmem_shape(rows, LANES, kind=jnp.float32),
            vmem_shape(features, width),
            vmem_shape(SLAB, features, kind=jnp.float32),
            vmem_shape(rows, features),
            vmem_shape(rows, width),
        ),
        in_specs=[VMEM if direct else ANYWHERE] * len(recv) + [ANYWHERE] * 2,
        out_specs=(VMEM,) * 10,
        scratch_shapes=[
            pltpu.VMEM((features, width), bf),
            pltpu.VMEM((mp_size, SLAB, features), bf),
            pltpu.SemaphoreType.DMA(()),
            pltpu.SemaphoreType.DMA((3, mp_size)),
            *staging[:1],
        ],
        compiler_params=params(14 + rows // 48),
        name="weight_grads",
    )(*inputs)
    near = swap(send, 1)

    tile = min(256, rows)
    chunk_rows = capacity * block_rows
    keep, *token_parts = pl.pallas_call(
        functools.partial(token_grad_kernel, (tile, chunk_rows, direct, scale)),
        out_shape=[
            part,
            *([vmem_shape(chunk_rows, features)] * dp_size if direct else [pltpu.HBM((rows, features), bf)]),
        ],
        in_specs=[VMEM] * 9,
        out_specs=[VMEM] * (1 + dp_size) if direct else [VMEM, ANYWHERE],
        scratch_shapes=[] if direct else [pltpu.VMEM((rows, features), bf), pltpu.SemaphoreType.DMA(())],
        compiler_params=params(12 + rows // 64),
        name="token_grads",
    )(*in_vmem(*kept))

    def add(place, extent, kind, name):
        return pl.pallas_call(
            functools.partial(add_kernel, place),
            out_shape=vmem_shape(2, *extent, kind=kind),
            in_specs=[VMEM] * 2,
            out_specs=VMEM,
            compiler_params=params(14),
            name=name,
        )(*in_vmem(keep, near))

    far = swap(add(1, (shard, width), bf, "far_add"), 2)
    own_sum = add(0, (shard, lang_local, bottleneck), jnp.float32, "own_add")
    if direct:
        backs = in_vmem(*swap_all(token_parts))
    else:
        backs = in_hbm(exchange(token_parts[0].reshape(slots, block_rows, features)))
    grad_shape = shape(shard, lang_local, bottleneck)
    token_grad, grad_up, grad_down = pl.pallas_call(
        functools.partial(tail_kernel, (capacity, full, direct)),
        out_shape=(shape(*tokens.shape), grad_shape, grad_shape),
        in_specs=[SMEM] + [VMEM] * 2 + [VMEM if direct else ANYWHERE] * len(backs),
        out_specs=(ANYWHERE,) * 3,
        scratch_shapes=[
            pltpu.VMEM((2, shard, lang_local, bottleneck), bf),
            pltpu.SemaphoreType.DMA((4,)),
            pltpu.SemaphoreType.DMA((slots,)),
            *([] if direct else [pltpu.VMEM((slots, block_rows, features), bf)]),
        ],
        compiler_params=params(8 + slots // 4),
        name="tail",
    )(source, *in_vmem(own_sum, far), *backs)
    return (token_grad, grad_down, grad_up)


def solution(mesh):
    placed = (
        P("dp", "mp", None),
        P("dp", "mp", None),
        P("dp"),
        P("dp"),
        P(),
        P("mp", "dp"),
        P("mp", "dp", None),
        P("mp", "dp", None),
    )
    return jax.shard_map(
        shards,
        mesh=mesh,
        in_specs=placed,
        out_specs=(P("dp", "mp", None), P("mp", "dp", None), P("mp", "dp", None)),
        check_vma=False,
    )
```

```python
import functools
import math

import jax
import jax.numpy as jnp
from jax import lax
from jax.experimental import pallas as pl
from jax.experimental.pallas import tpu as pltpu
from jax.sharding import PartitionSpec as P

SLAB = 16
LANES = 128
MIB = 1024 * 1024
PIECES = 4
OFFSETS = (0, 4, 1, 5, 2, 6, 3, 7)
ANYWHERE = pl.BlockSpec(memory_space=pl.ANY)
VMEM = pl.BlockSpec(memory_space=pltpu.VMEM)
SMEM = pl.BlockSpec(memory_space=pltpu.SMEM)


def params(mib):
    return pltpu.CompilerParams(vmem_limit_bytes=min(mib, 60) * MIB)


def start_all(copies):
    for copy in copies:
        copy.start()


def wait_all(copies):
    for copy in copies:
        copy.wait()


def load_kernel(down_hbm, up_hbm, down_ref, up_ref, sems):
    copies = [
        pltpu.make_async_copy(src, dst, sems.at[n])
        for n, (src, dst) in enumerate(((down_hbm, down_ref), (up_hbm, up_ref)))
    ]
    start_all(copies)
    wait_all(copies)


def pair_kernel(after_ref, own_hbm, core_hbm, out_ref, sems):
    size = own_hbm.shape[0]
    copies = [
        pltpu.make_async_copy(src, out_ref.at[pl.ds(n * size, size)], sems.at[n])
        for n, src in enumerate((own_hbm, core_hbm))
    ]
    start_all(copies)
    wait_all(copies)


def pack_kernel(dims, lang_hbm, count_hbm, slot_hbm, x_hbm, dy_hbm, *refs):
    dp_size, capacity, lang_local, full, direct = dims
    chunks, (source_ref, *scratch) = (refs[:dp_size], refs[dp_size:]) if direct else (None, refs[1:])
    block_count, block_rows, features = x_hbm.shape
    slots = dp_size * capacity
    halves = block_rows // SLAB
    x_buf, dy_buf, lang_ref, count_ref, slot_ref, taken_ref, sems, *scratch = scratch
    if not direct:
        out_hbm, (packed, out_sem) = refs[0], scratch
    loads = [
        pltpu.make_async_copy(src, dst, sems.at[n])
        for n, (src, dst) in enumerate(
            (
                (lang_hbm, lang_ref),
                (count_hbm, count_ref),
                (slot_hbm, slot_ref),
                (x_hbm, x_buf),
                (dy_hbm, dy_buf),
            )
        )
    ]
    start_all(loads)

    def clear_owner(owner, carry):
        taken_ref[owner] = 0
        return carry

    def clear_slot(slot, carry):
        source_ref[slot] = -1
        return carry

    lax.fori_loop(0, dp_size, clear_owner, 0, unroll=dp_size <= 8)
    if not full:
        lax.fori_loop(0, slots, clear_slot, 0)
    wait_all(loads[:3])

    def place(block, carry):
        owner = slot_ref[lang_ref[block]] // lang_local
        rank = taken_ref[owner]
        taken_ref[owner] = rank + 1
        source_ref[owner * capacity + rank] = block
        return carry

    lax.fori_loop(0, block_count, place, 0, unroll=True)
    wait_all(loads[3:])
    row_start = lax.axis_index("mp") * block_rows
    dy_groups = capacity * halves
    lane = lax.broadcasted_iota(jnp.int32, (SLAB, LANES), 1)

    def lanes_of(group):
        return pl.ds(group * features, features)

    def fill(out, block, place_in):
        live = count_ref[block] - row_start
        for half in range(halves):
            here = pl.ds(half * SLAB, SLAB)
            group = place_in * halves + half
            out[:, lanes_of(group)] = x_buf[block, here, :]
            rows = lax.broadcasted_iota(jnp.int32, (SLAB, features), 0) + half * SLAB
            piece = dy_buf[block, here, :].astype(jnp.float32)
            out[:, lanes_of(dy_groups + group)] = jnp.where(rows < live, piece, 0.0).astype(jnp.bfloat16)

    def blank(out, place_in):
        for half in range(halves):
            for base in (0, dy_groups):
                group = base + place_in * halves + half
                out[:, lanes_of(group)] = jnp.zeros((SLAB, features), jnp.bfloat16)

    def one_peer(out, peer):
        tags = jnp.zeros((SLAB, LANES), jnp.int32)
        for place_in in range(capacity):
            block = source_ref[peer * capacity + place_in]
            if full:
                fill(out, block, place_in)
            else:
                pl.when(block >= 0)(functools.partial(fill, out, block, place_in))
                pl.when(block < 0)(functools.partial(blank, out, place_in))
                block = jnp.maximum(block, 0)
            local = slot_ref[lang_ref[block]] % lang_local
            tags = jnp.where(lane // (LANES // capacity) == place_in, local, tags)
        out[:, pl.ds(2 * dy_groups * features, LANES)] = tags.astype(jnp.float32).astype(jnp.bfloat16)

    if direct:
        for offset, out in zip(direct, chunks):
            one_peer(out, lax.axis_index("dp") ^ offset)
    else:

        def send_peer(peer, carry):
            one_peer(packed.at[peer], peer)
            pltpu.make_async_copy(packed.at[peer], out_hbm.at[peer], out_sem).start()
            return carry

        lax.fori_loop(0, dp_size, send_peer, 0)
        pltpu.make_async_copy(packed, out_hbm, out_sem).wait()


def spread(values, second):
    return jnp.concatenate([jnp.where(second, 0.0, values), jnp.where(second, values, 0.0)], axis=1).astype(jnp.bfloat16)


def pick(values, second):
    half = values.shape[1] // 2
    return jnp.where(second, values[:, half:], values[:, :half])


def wide(column):
    return jnp.broadcast_to(column, (column.shape[0], LANES))


def gains_of(gain_ref, second):
    return jnp.where(second, gain_ref[1:2, :], gain_ref[0:1, :])


def normalize(values, second, gain_ref):
    values = values.astype(jnp.float32)
    row_mean = jnp.mean(values, axis=-1, keepdims=True)
    centered = values - row_mean
    inv_std = lax.rsqrt(jnp.mean(centered * centered, axis=-1, keepdims=True) + 1e-05)
    normed = (centered * inv_std * gains_of(gain_ref, second)).astype(jnp.bfloat16)
    return row_mean, inv_std, normed


def middle(masked, inner, second, up_ref):
    bell = 0.5 * (1.0 + lax.erf(inner * (1.0 / math.sqrt(2.0))))
    slope = bell + inner * jnp.exp(-0.5 * inner * inner) * (1.0 / math.sqrt(2.0 * math.pi))
    grad_act = pick(jnp.dot(masked, up_ref[...], preferred_element_type=jnp.float32), second)
    return spread(inner * bell, second), spread(grad_act * slope, second)


def backward(values, masked, row_mean, inv_std, second, grad_inner, gain_ref, down_ref):
    grad_normed = lax.dot_general(
        grad_inner, down_ref[...], (((1,), (1,)), ((), ())), preferred_element_type=jnp.float32
    )
    unit = (values.astype(jnp.float32) - row_mean) * inv_std
    scaled = grad_normed * gains_of(gain_ref, second)
    token_grad = masked.astype(jnp.float32) + inv_std * (
        scaled - jnp.mean(scaled, axis=-1, keepdims=True) - unit * jnp.mean(scaled * unit, axis=-1, keepdims=True)
    )
    return token_grad.astype(jnp.bfloat16)


def weight_grad_kernel(dims, *refs):
    capacity, mp_size, tile, scale, direct = dims
    source_count = len(direct) or 1
    sources, (pair_hbm, far_hbm), refs = refs[:source_count], refs[source_count:][:2], refs[source_count + 2 :]
    half = mp_size // 2
    send_refs, refs = refs[:half], refs[half:]
    x_buf, dy_buf, inner_buf, stats_buf, id_buf, down_ref, gain_ref, normed_buf, act_buf = refs[:9]
    up_ref, gain_buf, sems, weight_sems, *scratch = refs[9:]
    rows, features = x_buf.shape
    shard = features // mp_size
    first, then, later = [], [], []
    if direct:
        raw = sources
        chunks = len(direct)
    else:
        (raw,) = scratch
        chunks = raw.shape[0]
    groups = rows // (chunks * SLAB)
    split = groups * features
    if not direct:
        first.append(pltpu.make_async_copy(sources[0], raw, sems))
    size = pair_hbm.shape[0] // 2
    for offset in range(mp_size):
        weight, start = (pair_hbm, far_hbm)[offset // 2], offset % 2 * size
        here = pl.ds(pl.multiple_of((lax.axis_index("mp") ^ offset) * shard, shard), shard)
        for n, (group, src, dst) in enumerate(
            (
                (first, weight.at[pl.ds(start + 2 * shard, SLAB)], gain_buf.at[offset]),
                (then, weight.at[pl.ds(start, shard)], down_ref.at[here]),
                (later, weight.at[pl.ds(start + shard, shard)], up_ref.at[here]),
            )
        ):
            group.append(pltpu.make_async_copy(src, dst, weight_sems.at[n, offset]))
    start_all(first)
    start_all(then)
    start_all(later)
    wait_all(first)
    for offset in range(mp_size):
        here = pl.ds(pl.multiple_of((lax.axis_index("mp") ^ offset) * shard, shard), shard)
        gain_ref[:, here] = gain_buf[offset, :, pl.ds(0, shard)].astype(jnp.float32)
    tile_chunks = tile // (groups * SLAB)
    per_block = groups // capacity

    def chunk_of(step, chunk):
        return raw[chunk] if direct else raw.at[step * tile_chunks + chunk]

    def rows_of(step, base):
        return jnp.concatenate(
            [
                chunk_of(step, chunk)[:, pl.ds((base + group) * features, features)]
                for chunk in range(tile_chunks)
                for group in range(groups)
            ],
            axis=0,
        )

    def ids_of(step):
        pieces = []
        for chunk in range(tile_chunks):
            tags = chunk_of(step, chunk)[:, pl.ds(2 * split, LANES)].astype(jnp.float32)
            for group in range(groups):
                column = (group // per_block) * (LANES // capacity)
                pieces.append(wide(tags[:, column : column + 1]))
        return jnp.concatenate(pieces, axis=0)

    whole = rows == tile
    if not whole:
        wait_all(then + later)

    def one_tile(step, carry):
        here = pl.ds(pl.multiple_of(step * tile, tile), tile)
        ids = ids_of(step)
        id_buf[here, :] = ids
        second = ids[:, :1] > 0.5
        values = rows_of(step, 0)
        x_buf[here, :] = values
        row_mean, inv_std, normed = normalize(values, second, gain_ref)
        normed_buf[here, :] = normed
        stats_buf[here, :] = jnp.concatenate([wide(row_mean), wide(inv_std)], axis=1)
        if whole:
            wait_all(then)
        inner = pick(jnp.dot(normed_buf[here, :], down_ref[...], preferred_element_type=jnp.float32), second)
        if whole:
            wait_all(later)
        dy_buf[here, :] = rows_of(step, groups)
        act, grad_inner = middle(dy_buf[here, :], inner, second, up_ref)
        act_buf[here, :] = act
        inner_buf[here, :] = grad_inner
        return carry

    if whole:
        one_tile(0, 0)
    else:
        lax.fori_loop(0, rows // tile, one_tile, 0)
    products(dy_buf, act_buf, normed_buf, inner_buf, send_refs, 1, scale)


def products(dy_ref, act_ref, normed_ref, inner_ref, out_refs, first, scale):
    shard = out_refs[0].shape[1]
    for n, out_ref in enumerate(out_refs):
        here = pl.ds(pl.multiple_of((lax.axis_index("mp") ^ (2 * n + first)) * shard, shard), shard)
        for kind, (left, right) in enumerate(((dy_ref, act_ref), (normed_ref, inner_ref))):
            part = lax.dot_general(
                left[:, here], right[...], (((0,), (0,)), ((), ())), preferred_element_type=jnp.float32
            )
            out_ref[kind] = (part * scale).astype(jnp.bfloat16)


def token_grad_kernel(
    dims, x_ref, dy_ref, inner_ref, stats_ref, id_ref, down_ref, gain_ref, normed_ref, act_ref, *refs
):
    tile, chunk_rows, direct, scale, half = dims
    keep_refs, refs = refs[:half], refs[half:]
    rows = x_ref.shape[0]

    def part(here):
        stats = stats_ref[here, :]
        return backward(
            x_ref[here, :],
            dy_ref[here, :],
            stats[:, :1],
            stats[:, LANES : LANES + 1],
            id_ref[here, :][:, :1] > 0.5,
            inner_ref[here, :],
            gain_ref,
            down_ref,
        )

    if direct:
        for step in range(rows // tile):
            token_grad = part(pl.ds(step * tile, tile))
            for n in range(tile // chunk_rows):
                refs[step * (tile // chunk_rows) + n][...] = token_grad[n * chunk_rows : (n + 1) * chunk_rows]
        products(dy_ref, act_ref, normed_ref, inner_ref, keep_refs, 0, scale)
        return
    out_hbm, grad_buf, sem = refs

    def one_tile(step, carry):
        here = pl.ds(pl.multiple_of(step * tile, tile), tile)
        grad_buf[here, :] = part(here)
        pltpu.make_async_copy(grad_buf.at[here], out_hbm.at[here], sem).start()
        return carry

    lax.fori_loop(0, rows // tile, one_tile, 0)
    products(dy_ref, act_ref, normed_ref, inner_ref, keep_refs, 0, scale)
    pltpu.make_async_copy(grad_buf, out_hbm, sem).wait()


def add_kernel(keep_ref, near_ref, *refs):
    out_ref = refs[-1]
    for kind in range(keep_ref.shape[0]):
        total = keep_ref[kind].astype(jnp.float32) + near_ref[kind].astype(jnp.float32)
        out_ref[kind] = total.reshape(out_ref.shape[1:]).astype(out_ref.dtype)


def tail_kernel(dims, source_ref, own_ref, far_ref, *refs):
    capacity, full, direct = dims
    back_count = len(direct) or 1
    backs, (out_hbm, *grad_hbms, grad, sems, out_sems), buf = (
        refs[:back_count],
        refs[back_count : back_count + 6],
        refs[back_count + 6 :],
    )
    slots = out_sems.shape[0]
    block_rows = out_hbm.shape[1]
    half = slots // 2

    def store(slot, piece):
        if full:
            return pltpu.make_async_copy(piece, out_hbm.at[source_ref[slot]], out_sems.at[0])
        return pltpu.make_async_copy(piece, out_hbm.at[jnp.maximum(source_ref[slot], 0)], out_sems.at[slot])

    if direct:
        for offset, back in zip(direct, backs):
            for place_in in range(capacity):
                slot = (lax.axis_index("dp") ^ offset) * capacity + place_in
                store(slot, back.at[pl.ds(place_in * block_rows, block_rows)]).start()
    else:
        (buf,) = buf
        loads = [
            pltpu.make_async_copy(backs[0].at[pl.ds(n * half, half)], buf.at[pl.ds(n * half, half)], sems.at[n])
            for n in range(2)
        ]
        start_all(loads)
        for n, load in enumerate(loads):
            load.wait()
            for slot in range(n * half, (n + 1) * half):
                if full:
                    store(slot, buf.at[slot]).start()
                else:
                    pl.when(source_ref[slot] >= 0)(store(slot, buf.at[slot]).start)
    writes = []
    piece = grad.shape[1] // PIECES
    for n in range(PIECES):
        here = pl.ds(n * piece, piece)
        for kind, grad_hbm in enumerate(grad_hbms):
            total = own_ref[kind, here, :] + far_ref[kind, here, :].astype(jnp.float32)
            grad[kind, here] = total.reshape(piece, *grad.shape[2:]).astype(grad.dtype)
            writes.append(pltpu.make_async_copy(grad.at[kind, here], grad_hbm.at[here], sems.at[2 + PIECES * kind + n]))
            writes[-1].start()
    if full:
        pltpu.make_async_copy(out_hbm, out_hbm, out_sems.at[0]).wait()
    else:
        for slot in range(slots):
            pl.when(source_ref[slot] >= 0)(store(slot, buf.at[slot]).wait)
    wait_all(writes)


def shards(tokens, cotangent, block_lang, counts, slot_of, ln_gain, w_down, w_up):
    block_count, block_rows, features = tokens.shape
    dp_size = lax.axis_size("dp")
    mp_size = lax.axis_size("mp")
    lang_local, bottleneck = w_down.shape[1:]
    shard = w_down.shape[0]
    width = lang_local * bottleneck
    capacity = (block_count + dp_size - 1) // dp_size
    slots = dp_size * capacity
    full = slots == block_count
    halves = block_rows // SLAB
    groups = capacity * halves
    lanes = 2 * groups * features + LANES
    rows = slots * block_rows
    tile = min(512, rows)
    resident = rows <= tile
    bf = jnp.bfloat16

    def shape(*extent, kind=bf):
        return jax.ShapeDtypeStruct(extent, kind)

    def vmem_shape(*extent, kind=bf):
        return pltpu.VMEM(extent, kind) if resident else shape(*extent, kind=kind)

    def in_vmem(*arrays):
        return [pltpu.with_memory_space_constraint(array, pltpu.VMEM) if resident else array for array in arrays]

    def in_hbm(*arrays):
        return [pltpu.with_memory_space_constraint(array, pltpu.HBM) for array in arrays]

    def swap(array, bit):
        return lax.ppermute(array, "mp", [(i, i ^ bit) for i in range(mp_size)])

    def exchange(array):
        return lax.all_to_all(array, "dp", split_axis=0, concat_axis=0, tiled=True)

    def swap_all(chunks):
        return [
            lax.ppermute(chunk, "dp", [(i, i ^ offset) for i in range(dp_size)]) if offset else chunk
            for offset, chunk in zip(OFFSETS, chunks)
        ]

    direct = OFFSETS if resident and dp_size == len(OFFSETS) else ()
    chunk_shape = [vmem_shape(SLAB, lanes)] * dp_size if direct else [pltpu.HBM((dp_size, SLAB, lanes), bf)]
    staging = [] if direct else [pltpu.VMEM((dp_size, SLAB, lanes), bf), pltpu.SemaphoreType.DMA(())]
    *packed, source = pl.pallas_call(
        functools.partial(pack_kernel, (dp_size, capacity, lang_local, full, direct)),
        out_shape=(*chunk_shape, shape(slots, kind=jnp.int32)),
        in_specs=[ANYWHERE] * 5,
        out_specs=(*([VMEM] * dp_size if direct else [ANYWHERE]), SMEM),
        scratch_shapes=[
            pltpu.VMEM(tokens.shape, bf),
            pltpu.VMEM(cotangent.shape, bf),
            pltpu.SMEM(block_lang.shape, jnp.int32),
            pltpu.SMEM(counts.shape, jnp.int32),
            pltpu.SMEM(slot_of.shape, jnp.int32),
            pltpu.SMEM((dp_size,), jnp.int32),
            pltpu.SemaphoreType.DMA((5,)),
            *staging,
        ],
        compiler_params=params(8 + slots // 4),
        name="pack",
    )(*in_hbm(block_lang, counts, slot_of, tokens, cotangent))

    down_raw, up_raw = pl.pallas_call(
        load_kernel,
        out_shape=(vmem_shape(*w_down.shape), vmem_shape(*w_up.shape)),
        in_specs=[ANYWHERE] * 2,
        out_specs=(VMEM if resident else ANYWHERE,) * 2,
        scratch_shapes=[pltpu.SemaphoreType.DMA((2,))],
        compiler_params=params(2),
        name="load",
    )(*in_hbm(w_down, w_up))
    gain_part = jnp.pad(ln_gain.T, ((0, SLAB - lang_local), (0, width - shard)))
    own = jnp.concatenate([down_raw.reshape(shard, width), up_raw.reshape(shard, width), gain_part], axis=0)
    core = swap(own, 1)
    pair = pl.pallas_call(
        pair_kernel,
        out_shape=vmem_shape(2 * own.shape[0], width),
        in_specs=[SMEM] + [ANYWHERE] * 2,
        out_specs=VMEM if resident else ANYWHERE,
        scratch_shapes=[pltpu.SemaphoreType.DMA((2,))],
        compiler_params=params(2 if resident else 8),
        name="pair",
    )(source, own, core)
    pair_far = swap(pair, 2)

    if direct:
        recv = swap_all(packed)
    else:
        recv = [exchange(packed[0])]
    inputs = in_vmem(*recv, pair, pair_far) if direct else in_hbm(*recv, pair, pair_far)

    half = mp_size // 2
    part = vmem_shape(2, shard, width)
    scale = 1.0 / (block_rows * mp_size)
    results = pl.pallas_call(
        functools.partial(weight_grad_kernel, (capacity, mp_size, tile, scale, direct)),
        out_shape=(
            *[part] * half,
            vmem_shape(rows, features),
            vmem_shape(rows, features),
            vmem_shape(rows, width),
            vmem_shape(rows, 2 * LANES, kind=jnp.float32),
            vmem_shape(rows, LANES, kind=jnp.float32),
            vmem_shape(features, width),
            vmem_shape(SLAB, features, kind=jnp.float32),
            vmem_shape(rows, features),
            vmem_shape(rows, width),
        ),
        in_specs=[VMEM if direct else ANYWHERE] * len(recv) + [ANYWHERE] * 2,
        out_specs=(VMEM,) * (9 + half),
        scratch_shapes=[
            pltpu.VMEM((features, width), bf),
            pltpu.VMEM((mp_size, SLAB, features), bf),
            pltpu.SemaphoreType.DMA(()),
            pltpu.SemaphoreType.DMA((3, mp_size)),
            *staging[:1],
        ],
        compiler_params=params(14 + rows // 48),
        name="weight_grads",
    )(*inputs)
    kept = results[half:]
    near_far, near_own = swap(results[1], 1), swap(results[0], 1)

    tile = min(256, rows)
    chunk_rows = capacity * block_rows
    keep_own, keep_far, *token_parts = pl.pallas_call(
        functools.partial(token_grad_kernel, (tile, chunk_rows, direct, scale, half)),
        out_shape=[
            *[part] * half,
            *([vmem_shape(chunk_rows, features)] * dp_size if direct else [pltpu.HBM((rows, features), bf)]),
        ],
        in_specs=[VMEM] * 9,
        out_specs=[VMEM] * half + ([VMEM] * dp_size if direct else [ANYWHERE]),
        scratch_shapes=[] if direct else [pltpu.VMEM((rows, features), bf), pltpu.SemaphoreType.DMA(())],
        compiler_params=params(12 + rows // 64),
        name="token_grads",
    )(*in_vmem(*kept))

    def add(keep, near, extent, kind, name, *through):
        *through, result = pl.pallas_call(
            add_kernel,
            out_shape=(
                *[vmem_shape(*array.shape) for array in through],
                vmem_shape(2, *extent, kind=kind),
            ),
            in_specs=[VMEM] * 2 + [ANYWHERE] * len(through),
            out_specs=(*[ANYWHERE] * len(through), VMEM),
            input_output_aliases={2 + n: n for n in range(len(through))},
            compiler_params=params(14),
            name=name,
        )(*in_vmem(keep, near, *through))
        return result, *through

    (far_sum,) = add(keep_far, near_far, (shard, width), bf, "far_add")
    far = swap(far_sum, 2)
    own_sum, *sent = add(
        keep_own, near_own, (shard, width), jnp.float32, "own_add", *token_parts[1 if direct else 2 :]
    )
    token_parts = token_parts[:1] + sent
    if direct:
        backs = in_vmem(*swap_all(token_parts))
    else:
        backs = in_hbm(exchange(token_parts[0].reshape(slots, block_rows, features)))
    grad_shape = shape(shard, lang_local, bottleneck)
    token_grad, grad_up, grad_down = pl.pallas_call(
        functools.partial(tail_kernel, (capacity, full, direct)),
        out_shape=(shape(*tokens.shape), grad_shape, grad_shape),
        in_specs=[SMEM] + [VMEM] * 2 + [VMEM if direct else ANYWHERE] * len(backs),
        out_specs=(ANYWHERE,) * 3,
        scratch_shapes=[
            pltpu.VMEM((2, shard, lang_local, bottleneck), bf),
            pltpu.SemaphoreType.DMA((2 + 2 * PIECES,)),
            pltpu.SemaphoreType.DMA((slots,)),
            *([] if direct else [pltpu.VMEM((slots, block_rows, features), bf)]),
        ],
        compiler_params=params(8 + slots // 4),
        name="tail",
    )(source, *in_vmem(own_sum, far), *backs)
    return (token_grad, grad_down, grad_up)


def solution(mesh):
    placed = (
        P("dp", "mp", None),
        P("dp", "mp", None),
        P("dp"),
        P("dp"),
        P(),
        P("mp", "dp"),
        P("mp", "dp", None),
        P("mp", "dp", None),
    )
    return jax.shard_map(
        shards,
        mesh=mesh,
        in_specs=placed,
        out_specs=(P("dp", "mp", None), P("mp", "dp", None), P("mp", "dp", None)),
        check_vma=False,
    )
```

```python
import functools
import math

import jax
import jax.numpy as jnp
from jax import lax
from jax.experimental import pallas as pl
from jax.experimental.pallas import tpu as pltpu
from jax.sharding import PartitionSpec as P

SLAB = 16
LANES = 128
MIB = 1024 * 1024
PIECES = 4
OFFSETS = (0, 4, 2, 5, 1, 6, 3, 7)
RETURN_OFFSETS = (0, 4, 1, 5, 2, 6, 3, 7)
ANYWHERE = pl.BlockSpec(memory_space=pl.ANY)
VMEM = pl.BlockSpec(memory_space=pltpu.VMEM)
SMEM = pl.BlockSpec(memory_space=pltpu.SMEM)


def params(mib):
    return pltpu.CompilerParams(vmem_limit_bytes=min(mib, 60) * MIB)


def start_all(copies):
    for copy in copies:
        copy.start()


def wait_all(copies):
    for copy in copies:
        copy.wait()


def load_kernel(down_hbm, up_hbm, down_ref, up_ref, sems):
    copies = [
        pltpu.make_async_copy(src, dst, sems.at[n])
        for n, (src, dst) in enumerate(((down_hbm, down_ref), (up_hbm, up_ref)))
    ]
    start_all(copies)
    wait_all(copies)


def pair_kernel(after_ref, own_hbm, core_hbm, out_ref, sems):
    size = own_hbm.shape[0]
    copies = [
        pltpu.make_async_copy(src, out_ref.at[pl.ds(n * size, size)], sems.at[n])
        for n, src in enumerate((own_hbm, core_hbm))
    ]
    start_all(copies)
    wait_all(copies)


def pack_kernel(dims, lang_hbm, count_hbm, slot_hbm, x_hbm, dy_hbm, *refs):
    dp_size, capacity, lang_local, full, direct = dims
    chunks, (source_ref, *scratch) = (refs[:dp_size], refs[dp_size:]) if direct else (None, refs[1:])
    block_count, block_rows, features = x_hbm.shape
    slots = dp_size * capacity
    halves = block_rows // SLAB
    x_buf, dy_buf, lang_ref, count_ref, slot_ref, taken_ref, sems, *scratch = scratch
    if not direct:
        out_hbm, (packed, out_sem) = refs[0], scratch
    loads = [
        pltpu.make_async_copy(src, dst, sems.at[n])
        for n, (src, dst) in enumerate(
            (
                (lang_hbm, lang_ref),
                (count_hbm, count_ref),
                (slot_hbm, slot_ref),
                (x_hbm, x_buf),
                (dy_hbm, dy_buf),
            )
        )
    ]
    start_all(loads)

    def clear_owner(owner, carry):
        taken_ref[owner] = 0
        return carry

    def clear_slot(slot, carry):
        source_ref[slot] = -1
        return carry

    lax.fori_loop(0, dp_size, clear_owner, 0, unroll=dp_size <= 8)
    if not full:
        lax.fori_loop(0, slots, clear_slot, 0)
    wait_all(loads[:3])

    def place(block, carry):
        owner = slot_ref[lang_ref[block]] // lang_local
        rank = taken_ref[owner]
        taken_ref[owner] = rank + 1
        source_ref[owner * capacity + rank] = block
        return carry

    lax.fori_loop(0, block_count, place, 0, unroll=True)
    wait_all(loads[3:])
    row_start = lax.axis_index("mp") * block_rows
    dy_groups = capacity * halves
    lane = lax.broadcasted_iota(jnp.int32, (SLAB, LANES), 1)

    def lanes_of(group):
        return pl.ds(group * features, features)

    def fill(out, block, place_in):
        live = count_ref[block] - row_start
        for half in range(halves):
            here = pl.ds(half * SLAB, SLAB)
            group = place_in * halves + half
            out[:, lanes_of(group)] = x_buf[block, here, :]
            rows = lax.broadcasted_iota(jnp.int32, (SLAB, features), 0) + half * SLAB
            piece = dy_buf[block, here, :].astype(jnp.float32)
            out[:, lanes_of(dy_groups + group)] = jnp.where(rows < live, piece, 0.0).astype(jnp.bfloat16)

    def blank(out, place_in):
        for half in range(halves):
            for base in (0, dy_groups):
                group = base + place_in * halves + half
                out[:, lanes_of(group)] = jnp.zeros((SLAB, features), jnp.bfloat16)

    def one_peer(out, peer):
        tags = jnp.zeros((SLAB, LANES), jnp.int32)
        for place_in in range(capacity):
            block = source_ref[peer * capacity + place_in]
            if full:
                fill(out, block, place_in)
            else:
                pl.when(block >= 0)(functools.partial(fill, out, block, place_in))
                pl.when(block < 0)(functools.partial(blank, out, place_in))
                block = jnp.maximum(block, 0)
            local = slot_ref[lang_ref[block]] % lang_local
            tags = jnp.where(lane // (LANES // capacity) == place_in, local, tags)
        out[:, pl.ds(2 * dy_groups * features, LANES)] = tags.astype(jnp.float32).astype(jnp.bfloat16)

    if direct:
        for offset, out in zip(direct, chunks):
            one_peer(out, lax.axis_index("dp") ^ offset)
    else:

        def send_peer(peer, carry):
            one_peer(packed.at[peer], peer)
            pltpu.make_async_copy(packed.at[peer], out_hbm.at[peer], out_sem).start()
            return carry

        lax.fori_loop(0, dp_size, send_peer, 0)
        pltpu.make_async_copy(packed, out_hbm, out_sem).wait()


def spread(values, second):
    return jnp.concatenate([jnp.where(second, 0.0, values), jnp.where(second, values, 0.0)], axis=1).astype(jnp.bfloat16)


def pick(values, second):
    half = values.shape[1] // 2
    return jnp.where(second, values[:, half:], values[:, :half])


def wide(column):
    return jnp.broadcast_to(column, (column.shape[0], LANES))


def gains_of(gain_ref, second):
    return jnp.where(second, gain_ref[1:2, :], gain_ref[0:1, :])


def normalize(values, second, gain_ref):
    values = values.astype(jnp.float32)
    row_mean = jnp.mean(values, axis=-1, keepdims=True)
    centered = values - row_mean
    inv_std = lax.rsqrt(jnp.mean(centered * centered, axis=-1, keepdims=True) + 1e-05)
    normed = (centered * inv_std * gains_of(gain_ref, second)).astype(jnp.bfloat16)
    return row_mean, inv_std, normed


def middle(masked, inner, second, up_ref):
    bell = 0.5 * (1.0 + lax.erf(inner * (1.0 / math.sqrt(2.0))))
    slope = bell + inner * jnp.exp(-0.5 * inner * inner) * (1.0 / math.sqrt(2.0 * math.pi))
    grad_act = pick(jnp.dot(masked, up_ref[...], preferred_element_type=jnp.float32), second)
    return spread(inner * bell, second), spread(grad_act * slope, second)


def backward(values, masked, row_mean, inv_std, second, grad_inner, gain_ref, down_ref):
    grad_normed = lax.dot_general(
        grad_inner, down_ref[...], (((1,), (1,)), ((), ())), preferred_element_type=jnp.float32
    )
    unit = (values.astype(jnp.float32) - row_mean) * inv_std
    scaled = grad_normed * gains_of(gain_ref, second)
    token_grad = masked.astype(jnp.float32) + inv_std * (
        scaled - jnp.mean(scaled, axis=-1, keepdims=True) - unit * jnp.mean(scaled * unit, axis=-1, keepdims=True)
    )
    return token_grad.astype(jnp.bfloat16)


def weight_grad_kernel(dims, *refs):
    capacity, mp_size, tile, scale, direct = dims
    source_count = len(direct) or 1
    sources, (pair_hbm, far_hbm), refs = refs[:source_count], refs[source_count:][:2], refs[source_count + 2 :]
    half = mp_size // 2
    send_refs, refs = refs[:half], refs[half:]
    x_buf, dy_buf, inner_buf, stats_buf, id_buf, down_ref, gain_ref, normed_buf, act_buf = refs[:9]
    up_ref, gain_buf, sems, weight_sems, *scratch = refs[9:]
    rows, features = x_buf.shape
    shard = features // mp_size
    first, then, later = [], [], []
    if direct:
        raw = sources
        chunks = len(direct)
    else:
        (raw,) = scratch
        chunks = raw.shape[0]
    groups = rows // (chunks * SLAB)
    split = groups * features
    if not direct:
        first.append(pltpu.make_async_copy(sources[0], raw, sems))
    size = pair_hbm.shape[0] // 2
    for offset in range(mp_size):
        weight, start = (pair_hbm, far_hbm)[offset // 2], offset % 2 * size
        here = pl.ds(pl.multiple_of((lax.axis_index("mp") ^ offset) * shard, shard), shard)
        for n, (group, src, dst) in enumerate(
            (
                (first, weight.at[pl.ds(start + 2 * shard, SLAB)], gain_buf.at[offset]),
                (then, weight.at[pl.ds(start, shard)], down_ref.at[here]),
                (later, weight.at[pl.ds(start + shard, shard)], up_ref.at[here]),
            )
        ):
            group.append(pltpu.make_async_copy(src, dst, weight_sems.at[n, offset]))
    start_all(first)
    start_all(then)
    start_all(later)
    wait_all(first)
    for offset in range(mp_size):
        here = pl.ds(pl.multiple_of((lax.axis_index("mp") ^ offset) * shard, shard), shard)
        gain_ref[:, here] = gain_buf[offset, :, pl.ds(0, shard)].astype(jnp.float32)
    tile_chunks = tile // (groups * SLAB)
    per_block = groups // capacity

    def chunk_of(step, chunk):
        return raw[chunk] if direct else raw.at[step * tile_chunks + chunk]

    def rows_of(step, base):
        return jnp.concatenate(
            [
                chunk_of(step, chunk)[:, pl.ds((base + group) * features, features)]
                for chunk in range(tile_chunks)
                for group in range(groups)
            ],
            axis=0,
        )

    def ids_of(step):
        pieces = []
        for chunk in range(tile_chunks):
            tags = chunk_of(step, chunk)[:, pl.ds(2 * split, LANES)].astype(jnp.float32)
            for group in range(groups):
                column = (group // per_block) * (LANES // capacity)
                pieces.append(wide(tags[:, column : column + 1]))
        return jnp.concatenate(pieces, axis=0)

    whole = rows == tile
    if not whole:
        wait_all(then + later)

    def one_tile(step, carry):
        here = pl.ds(pl.multiple_of(step * tile, tile), tile)
        ids = ids_of(step)
        id_buf[here, :] = ids
        second = ids[:, :1] > 0.5
        values = rows_of(step, 0)
        x_buf[here, :] = values
        row_mean, inv_std, normed = normalize(values, second, gain_ref)
        normed_buf[here, :] = normed
        stats_buf[here, :] = jnp.concatenate([wide(row_mean), wide(inv_std)], axis=1)
        if whole:
            wait_all(then)
        inner = pick(jnp.dot(normed_buf[here, :], down_ref[...], preferred_element_type=jnp.float32), second)
        if whole:
            wait_all(later)
        dy_buf[here, :] = rows_of(step, groups)
        act, grad_inner = middle(dy_buf[here, :], inner, second, up_ref)
        act_buf[here, :] = act
        inner_buf[here, :] = grad_inner
        return carry

    if whole:
        one_tile(0, 0)
    else:
        lax.fori_loop(0, rows // tile, one_tile, 0)
    products(dy_buf, act_buf, normed_buf, inner_buf, send_refs, 1, scale)


def products(dy_ref, act_ref, normed_ref, inner_ref, out_refs, first, scale):
    shard = out_refs[0].shape[1]
    for n, out_ref in enumerate(out_refs):
        here = pl.ds(pl.multiple_of((lax.axis_index("mp") ^ (2 * n + first)) * shard, shard), shard)
        for kind, (left, right) in enumerate(((dy_ref, act_ref), (normed_ref, inner_ref))):
            part = lax.dot_general(
                left[:, here], right[...], (((0,), (0,)), ((), ())), preferred_element_type=jnp.float32
            )
            out_ref[kind] = (part * scale).astype(jnp.bfloat16)


def token_grad_kernel(
    dims, x_ref, dy_ref, inner_ref, stats_ref, id_ref, down_ref, gain_ref, normed_ref, act_ref, *refs
):
    tile, chunk_rows, direct, scale, half = dims
    keep_refs, refs = refs[:half], refs[half:]
    rows = x_ref.shape[0]

    def part(here):
        stats = stats_ref[here, :]
        return backward(
            x_ref[here, :],
            dy_ref[here, :],
            stats[:, :1],
            stats[:, LANES : LANES + 1],
            id_ref[here, :][:, :1] > 0.5,
            inner_ref[here, :],
            gain_ref,
            down_ref,
        )

    if direct:
        for step in range(rows // tile):
            token_grad = part(pl.ds(step * tile, tile))
            for n in range(tile // chunk_rows):
                refs[step * (tile // chunk_rows) + n][...] = token_grad[n * chunk_rows : (n + 1) * chunk_rows]
        products(dy_ref, act_ref, normed_ref, inner_ref, keep_refs, 0, scale)
        return
    out_hbm, grad_buf, sem = refs

    def one_tile(step, carry):
        here = pl.ds(pl.multiple_of(step * tile, tile), tile)
        grad_buf[here, :] = part(here)
        pltpu.make_async_copy(grad_buf.at[here], out_hbm.at[here], sem).start()
        return carry

    lax.fori_loop(0, rows // tile, one_tile, 0)
    products(dy_ref, act_ref, normed_ref, inner_ref, keep_refs, 0, scale)
    pltpu.make_async_copy(grad_buf, out_hbm, sem).wait()


def add_kernel(keep_ref, near_ref, *refs):
    out_ref = refs[-1]
    for kind in range(keep_ref.shape[0]):
        total = keep_ref[kind].astype(jnp.float32) + near_ref[kind].astype(jnp.float32)
        out_ref[kind] = total.reshape(out_ref.shape[1:]).astype(out_ref.dtype)


def tail_kernel(dims, source_ref, own_ref, far_ref, *refs):
    capacity, full, direct = dims
    back_count = len(direct) or 1
    backs, (out_hbm, *grad_hbms, grad, sems, out_sems), buf = (
        refs[:back_count],
        refs[back_count : back_count + 6],
        refs[back_count + 6 :],
    )
    slots = out_sems.shape[0]
    block_rows = out_hbm.shape[1]
    half = slots // 2

    def store(slot, piece):
        if full:
            return pltpu.make_async_copy(piece, out_hbm.at[source_ref[slot]], out_sems.at[0])
        return pltpu.make_async_copy(piece, out_hbm.at[jnp.maximum(source_ref[slot], 0)], out_sems.at[slot])

    if direct:
        for offset, back in zip(direct, backs):
            for place_in in range(capacity):
                slot = (lax.axis_index("dp") ^ offset) * capacity + place_in
                store(slot, back.at[pl.ds(place_in * block_rows, block_rows)]).start()
    else:
        (buf,) = buf
        loads = [
            pltpu.make_async_copy(backs[0].at[pl.ds(n * half, half)], buf.at[pl.ds(n * half, half)], sems.at[n])
            for n in range(2)
        ]
        start_all(loads)
        for n, load in enumerate(loads):
            load.wait()
            for slot in range(n * half, (n + 1) * half):
                if full:
                    store(slot, buf.at[slot]).start()
                else:
                    pl.when(source_ref[slot] >= 0)(store(slot, buf.at[slot]).start)
    writes = []
    piece = grad.shape[1] // PIECES
    for n in range(PIECES):
        here = pl.ds(n * piece, piece)
        for kind, grad_hbm in enumerate(grad_hbms):
            total = own_ref[kind, here, :] + far_ref[kind, here, :].astype(jnp.float32)
            grad[kind, here] = total.reshape(piece, *grad.shape[2:]).astype(grad.dtype)
            writes.append(pltpu.make_async_copy(grad.at[kind, here], grad_hbm.at[here], sems.at[2 + PIECES * kind + n]))
            writes[-1].start()
    if full:
        pltpu.make_async_copy(out_hbm, out_hbm, out_sems.at[0]).wait()
    else:
        for slot in range(slots):
            pl.when(source_ref[slot] >= 0)(store(slot, buf.at[slot]).wait)
    wait_all(writes)


def shards(tokens, cotangent, block_lang, counts, slot_of, ln_gain, w_down, w_up):
    block_count, block_rows, features = tokens.shape
    dp_size = lax.axis_size("dp")
    mp_size = lax.axis_size("mp")
    lang_local, bottleneck = w_down.shape[1:]
    shard = w_down.shape[0]
    width = lang_local * bottleneck
    capacity = (block_count + dp_size - 1) // dp_size
    slots = dp_size * capacity
    full = slots == block_count
    halves = block_rows // SLAB
    groups = capacity * halves
    lanes = 2 * groups * features + LANES
    rows = slots * block_rows
    tile = min(512, rows)
    resident = rows <= tile
    bf = jnp.bfloat16

    def shape(*extent, kind=bf):
        return jax.ShapeDtypeStruct(extent, kind)

    def vmem_shape(*extent, kind=bf):
        return pltpu.VMEM(extent, kind) if resident else shape(*extent, kind=kind)

    def in_vmem(*arrays):
        return [pltpu.with_memory_space_constraint(array, pltpu.VMEM) if resident else array for array in arrays]

    def in_hbm(*arrays):
        return [pltpu.with_memory_space_constraint(array, pltpu.HBM) for array in arrays]

    def swap(array, bit):
        return lax.ppermute(array, "mp", [(i, i ^ bit) for i in range(mp_size)])

    def exchange(array):
        return lax.all_to_all(array, "dp", split_axis=0, concat_axis=0, tiled=True)

    def swap_all(chunks):
        return [
            lax.ppermute(chunk, "dp", [(i, i ^ offset) for i in range(dp_size)]) if offset else chunk
            for offset, chunk in zip(OFFSETS, chunks)
        ]

    direct = OFFSETS if resident and dp_size == len(OFFSETS) else ()
    chunk_shape = [vmem_shape(SLAB, lanes)] * dp_size if direct else [pltpu.HBM((dp_size, SLAB, lanes), bf)]
    staging = [] if direct else [pltpu.VMEM((dp_size, SLAB, lanes), bf), pltpu.SemaphoreType.DMA(())]
    *packed, source = pl.pallas_call(
        functools.partial(pack_kernel, (dp_size, capacity, lang_local, full, direct)),
        out_shape=(*chunk_shape, shape(slots, kind=jnp.int32)),
        in_specs=[ANYWHERE] * 5,
        out_specs=(*([VMEM] * dp_size if direct else [ANYWHERE]), SMEM),
        scratch_shapes=[
            pltpu.VMEM(tokens.shape, bf),
            pltpu.VMEM(cotangent.shape, bf),
            pltpu.SMEM(block_lang.shape, jnp.int32),
            pltpu.SMEM(counts.shape, jnp.int32),
            pltpu.SMEM(slot_of.shape, jnp.int32),
            pltpu.SMEM((dp_size,), jnp.int32),
            pltpu.SemaphoreType.DMA((5,)),
            *staging,
        ],
        compiler_params=params(8 + slots // 4),
        name="pack",
    )(*in_hbm(block_lang, counts, slot_of, tokens, cotangent))

    down_raw, up_raw = pl.pallas_call(
        load_kernel,
        out_shape=(vmem_shape(*w_down.shape), vmem_shape(*w_up.shape)),
        in_specs=[ANYWHERE] * 2,
        out_specs=(VMEM if resident else ANYWHERE,) * 2,
        scratch_shapes=[pltpu.SemaphoreType.DMA((2,))],
        compiler_params=params(2),
        name="load",
    )(*in_hbm(w_down, w_up))
    gain_part = jnp.pad(ln_gain.T, ((0, SLAB - lang_local), (0, width - shard)))
    own = jnp.concatenate([down_raw.reshape(shard, width), up_raw.reshape(shard, width), gain_part], axis=0)
    core = swap(own, 1)
    pair = pl.pallas_call(
        pair_kernel,
        out_shape=vmem_shape(2 * own.shape[0], width),
        in_specs=[SMEM] + [ANYWHERE] * 2,
        out_specs=VMEM if resident else ANYWHERE,
        scratch_shapes=[pltpu.SemaphoreType.DMA((2,))],
        compiler_params=params(2 if resident else 8),
        name="pair",
    )(source, own, core)
    pair_far = swap(pair, 2)

    if direct:
        recv = swap_all(packed)
    else:
        recv = [exchange(packed[0])]
    inputs = in_vmem(*recv, pair, pair_far) if direct else in_hbm(*recv, pair, pair_far)

    half = mp_size // 2
    part = vmem_shape(2, shard, width)
    scale = 1.0 / (block_rows * mp_size)
    results = pl.pallas_call(
        functools.partial(weight_grad_kernel, (capacity, mp_size, tile, scale, direct)),
        out_shape=(
            *[part] * half,
            vmem_shape(rows, features),
            vmem_shape(rows, features),
            vmem_shape(rows, width),
            vmem_shape(rows, 2 * LANES, kind=jnp.float32),
            vmem_shape(rows, LANES, kind=jnp.float32),
            vmem_shape(features, width),
            vmem_shape(SLAB, features, kind=jnp.float32),
            vmem_shape(rows, features),
            vmem_shape(rows, width),
        ),
        in_specs=[VMEM if direct else ANYWHERE] * len(recv) + [ANYWHERE] * 2,
        out_specs=(VMEM,) * (9 + half),
        scratch_shapes=[
            pltpu.VMEM((features, width), bf),
            pltpu.VMEM((mp_size, SLAB, features), bf),
            pltpu.SemaphoreType.DMA(()),
            pltpu.SemaphoreType.DMA((3, mp_size)),
            *staging[:1],
        ],
        compiler_params=params(14 + rows // 48),
        name="weight_grads",
    )(*inputs)
    kept = results[half:]
    near_far, near_own = swap(results[1], 1), swap(results[0], 1)

    tile = min(256, rows)
    chunk_rows = capacity * block_rows
    keep_own, keep_far, *token_parts = pl.pallas_call(
        functools.partial(token_grad_kernel, (tile, chunk_rows, direct, scale, half)),
        out_shape=[
            *[part] * half,
            *([vmem_shape(chunk_rows, features)] * dp_size if direct else [pltpu.HBM((rows, features), bf)]),
        ],
        in_specs=[VMEM] * 9,
        out_specs=[VMEM] * half + ([VMEM] * dp_size if direct else [ANYWHERE]),
        scratch_shapes=[] if direct else [pltpu.VMEM((rows, features), bf), pltpu.SemaphoreType.DMA(())],
        compiler_params=params(12 + rows // 64),
        name="token_grads",
    )(*in_vmem(*kept))

    def add(keep, near, extent, kind, name, *through):
        *through, result = pl.pallas_call(
            add_kernel,
            out_shape=(
                *[vmem_shape(*array.shape) for array in through],
                vmem_shape(2, *extent, kind=kind),
            ),
            in_specs=[VMEM] * 2 + [ANYWHERE] * len(through),
            out_specs=(*[ANYWHERE] * len(through), VMEM),
            input_output_aliases={2 + n: n for n in range(len(through))},
            compiler_params=params(14),
            name=name,
        )(*in_vmem(keep, near, *through))
        return result, *through

    (far_sum,) = add(keep_far, near_far, (shard, width), bf, "far_add")
    far = swap(far_sum, 2)
    own_sum, *sent = add(
        keep_own, near_own, (shard, width), jnp.float32, "own_add", *token_parts[1 if direct else 2 :]
    )
    token_parts = token_parts[:1] + sent
    if direct:
        home = dict(zip(OFFSETS, swap_all(token_parts)))
        backs = in_vmem(*[home[offset] for offset in RETURN_OFFSETS])
    else:
        backs = in_hbm(exchange(token_parts[0].reshape(slots, block_rows, features)))
    grad_shape = shape(shard, lang_local, bottleneck)
    token_grad, grad_up, grad_down = pl.pallas_call(
        functools.partial(tail_kernel, (capacity, full, RETURN_OFFSETS if direct else ())),
        out_shape=(shape(*tokens.shape), grad_shape, grad_shape),
        in_specs=[SMEM] + [VMEM] * 2 + [VMEM if direct else ANYWHERE] * len(backs),
        out_specs=(ANYWHERE,) * 3,
        scratch_shapes=[
            pltpu.VMEM((2, shard, lang_local, bottleneck), bf),
            pltpu.SemaphoreType.DMA((2 + 2 * PIECES,)),
            pltpu.SemaphoreType.DMA((slots,)),
            *([] if direct else [pltpu.VMEM((slots, block_rows, features), bf)]),
        ],
        compiler_params=params(8 + slots // 4),
        name="tail",
    )(source, *in_vmem(own_sum, far), *backs)
    return (token_grad, grad_down, grad_up)


def solution(mesh):
    placed = (
        P("dp", "mp", None),
        P("dp", "mp", None),
        P("dp"),
        P("dp"),
        P(),
        P("mp", "dp"),
        P("mp", "dp", None),
        P("mp", "dp", None),
    )
    return jax.shard_map(
        shards,
        mesh=mesh,
        in_specs=placed,
        out_specs=(P("dp", "mp", None), P("mp", "dp", None), P("mp", "dp", None)),
        check_vma=False,
    )
```
